256 devices in a mesh: lat: 32 (over z, x), lon: 8 (over y, core).
Axes of the slice: x: 4, y: 4, z: 8, core: 2. Of those that a mesh axis runs over, the one named last changes fastest.
Arguments:
- state_grid: bfloat16 [512, 1440, 256], P('lat', 'lon'), may hold values from -6 to 6
- legendre: bfloat16 [512, 512, 512], P('lat'), may hold values from -0.25 to 0.25
- quad_weights: float32 [512], replicated, may hold values from 0.5 to 2
- spectral_gain: float32 [2, 512, 256], replicated, may hold values from -4 to 4
- skip_weight: bfloat16 [256, 256], replicated, may hold values from -0.375 to 0.375
- out_weight: bfloat16 [256, 256], replicated, may hold values from -0.375 to 0.375
- assignment: int32 [512], replicated, may hold values from 0 to 511, each once
- tile_mask: int32 [4, 4], replicated, may hold values from 0 to 1, as said below
Outputs:
- block_out: bfloat16 [512, 1440, 256], P('lat', 'lon')
The draws below stay inside these ranges and needn't reach their ends.
Inputs may be any that keep to these rules, and one draw needn't show every extreme that they name: `assignment`: each wave number from 0 to 511 appears once. `tile_mask`: tiles whose degree block lies below the wave-number block are 0; diagonal tiles are 1.
All inputs are finite; a program needn't handle non-finite values.
Results may differ from the reference program's by a relative error of at most 0.01.
Values may be sent and summed in bfloat16 or wider, within the bound.
A program may use at most 128 MiB of HBM per device.

```python
import math
import jax
import jax.numpy as jnp
from jax import lax

C = 256
NLON = 1440
MMAX = 512
LMAX = 512
LBLK = 128
NLAT = 512


def draw_tile_mask(key, part):
    key = jax.random.fold_in(key, 7)
    mode_blocks = MMAX // LBLK
    degree_blocks = LMAX // LBLK
    coins = jax.random.randint(key, (mode_blocks, degree_blocks), 0, 4)
    row_ids = lax.broadcasted_iota(jnp.int32, (mode_blocks, degree_blocks), 0)
    col_ids = lax.broadcasted_iota(jnp.int32, (mode_blocks, degree_blocks), 1)
    alive = (col_ids >= row_ids) & ((col_ids == row_ids) | (coins > 0))
    return alive.astype(jnp.int32)


def block_levels(rng, shape, cuts, smallest, largest):
    level, own = 1.0, jax.random.fold_in(rng, 6)
    for position, blocks in cuts:
        draws = jnp.exp(jax.random.uniform(jax.random.fold_in(own, position), (blocks,), jnp.float32, smallest / len(cuts), largest / len(cuts)))
        level = level * jnp.repeat(draws, shape[position] // blocks).reshape([-1 if axis == position else 1 for axis in range(len(shape))])
    return level


def gaussian(key, shape, spread, most, split=(), held_as=jnp.bfloat16):
    array = spread * jax.random.normal(key, shape, jnp.float32)
    if split:
        array = array * block_levels(key, shape, split, -0.22, 0.18)
    return jnp.clip(array, -most, most).astype(held_as)


def setup_inputs(seed: int = 0) -> dict:
    keys = jax.random.split(jax.random.key(seed), 9)
    return {
        "state_grid": gaussian(keys[0], (NLAT, NLON, C), 1.0, 6.0, ((0, 32), (1, 8))),
        "legendre": gaussian(keys[1], (MMAX, LMAX, NLAT), NLAT ** -0.5, 0.25, ((0, 32),)),
        "quad_weights": jnp.clip(jnp.exp(jax.random.uniform(keys[2], (NLAT,), jnp.float32, math.log(0.5), math.log(2.0))), 0.5, 2.0),
        "spectral_gain": gaussian(keys[3], (2, LMAX, C), 0.7, 4.0, (), jnp.float32),
        "skip_weight": gaussian(keys[4], (C, C), C ** -0.5, 0.375),
        "out_weight": gaussian(keys[5], (C, C), C ** -0.5, 0.375),
        "assignment": jax.random.permutation(keys[6], MMAX).astype(jnp.int32),
        "tile_mask": draw_tile_mask(jax.random.fold_in(keys[8], 71), 0),
    }


def fourier_angles(mode_ids, length):
    longitudes = jnp.arange(length, dtype=jnp.int32)
    residue = (longitudes[:, None] * mode_ids[None, :].astype(jnp.int32)) % length
    angles = residue.astype(jnp.float32) * (2.0 * math.pi / length)
    return jnp.cos(angles), jnp.sin(angles)


def forward_table(mode_ids, length):
    cosine, sine_part = fourier_angles(mode_ids, length)
    return (jnp.stack([cosine, -sine_part], axis=-1) / length).astype(jnp.bfloat16)


def inverse_table(mode_ids, length):
    cosine, sine_part = fourier_angles(mode_ids, length)
    doubling = jnp.where(mode_ids == 0, 1.0, 2.0).astype(jnp.float32)
    return jnp.stack([(cosine * doubling).T, (-sine_part * doubling).T], axis=1).astype(jnp.bfloat16)


def apply_gain(coefficient, gain_pair):
    real_part = coefficient[..., 0, :]
    imag_part = coefficient[..., 1, :]
    real_out = gain_pair[0] * real_part - gain_pair[1] * imag_part
    imag_out = gain_pair[0] * imag_part + gain_pair[1] * real_part
    return jnp.stack([real_out, imag_out], axis=-2).astype(jnp.bfloat16)


def mix_channels(state_grid, spatial, skip_weight, out_weight):
    skipped = jnp.dot(state_grid, skip_weight, preferred_element_type=jnp.float32)
    activated = jax.nn.gelu(spatial.astype(jnp.float32) + skipped, approximate=True).astype(jnp.bfloat16)
    mixed = jnp.dot(activated, out_weight, preferred_element_type=jnp.float32)
    return (state_grid.astype(jnp.float32) + mixed).astype(jnp.bfloat16)


def reference(state_grid, legendre, quad_weights, spectral_gain, skip_weight, out_weight, assignment, tile_mask):
    table_f = forward_table(assignment, NLON).astype(jnp.float32)
    fourier = jnp.einsum('anc,nkp->akpc', state_grid.astype(jnp.float32), table_f).astype(jnp.bfloat16)
    weighted = (quad_weights[:, None, None, None] * fourier.astype(jnp.float32)).astype(jnp.bfloat16)
    tile_rows = tile_mask[assignment // LBLK]
    live_mask = jnp.repeat(tile_rows, LBLK, axis=1).astype(jnp.float32)
    group_size = 64
    groups = MMAX // group_size
    basis_groups = legendre.reshape(groups, group_size, LMAX, NLAT)
    data_groups = jnp.moveaxis(weighted, 1, 0).reshape(groups, group_size, NLAT, 2, C)
    live_groups = live_mask.reshape(groups, group_size, LMAX)

    def one_group(members):
        basis_part, data_part, live_part = members
        basis_wide = basis_part.astype(jnp.float32)
        coefficient = jnp.einsum('kln,knpc->klpc', basis_wide, data_part.astype(jnp.float32))
        coefficient = coefficient * live_part[:, :, None, None]
        filtered = apply_gain(coefficient, spectral_gain)
        return jnp.einsum('kln,klpc->knpc', basis_wide, filtered.astype(jnp.float32)).astype(jnp.bfloat16)

    synthesis = lax.map(one_group, (basis_groups, data_groups, live_groups)).reshape(MMAX, NLAT, 2, C)
    table_i = inverse_table(assignment, NLON).astype(jnp.float32)
    spatial = jnp.einsum('knpc,kpm->nmc', synthesis.astype(jnp.float32), table_i).astype(jnp.bfloat16)
    return mix_channels(state_grid, spatial, skip_weight, out_weight)
```

```python
import functools
import math

import jax
import jax.numpy as jnp
import numpy as np
from jax import lax
from jax.experimental import pallas as pl
from jax.experimental.pallas import tpu as pltpu
from jax.sharding import PartitionSpec as P

MESH = pl.DeviceIdType.MESH
F32 = jnp.float32
BF16 = jnp.bfloat16

NLAT, NLON, C = 512, 1440, 256
MODES, LEVELS, LBLK = 512, 512, 128
NLATDEV, NLONDEV = 32, 8
LATS = NLAT // NLATDEV
ROWS = NLON // NLONDEV
PADDED = 192
LONS = PADDED * NLONDEV
KS = MODES // NLATDEV
CW = C // NLONDEV
GROUPS = 4
LG = LATS // GROUPS
LANES = LG * CW
PAIRS = KS // 2


def base_tables():
    m = np.arange(MODES, dtype=np.int64)
    n = np.arange(NLON, dtype=np.int64)
    angles = ((n[:, None] * m[None, :]) % NLON) * (2.0 * math.pi / NLON)
    cosine, sine = np.cos(angles), np.sin(angles)
    forward = np.zeros((2, MODES, NLONDEV, PADDED), np.float32)
    forward[0, :, :, :ROWS] = (cosine / NLON).T.reshape(MODES, NLONDEV, ROWS)
    forward[1, :, :, :ROWS] = (-sine / NLON).T.reshape(MODES, NLONDEV, ROWS)
    weight = np.where(m == 0, 1.0, 2.0)[None, :]
    inverse = np.zeros((NLONDEV, PADDED, 2, MODES), np.float32)
    inverse[:, :ROWS, 0] = (cosine * weight).reshape(NLONDEV, ROWS, MODES)
    inverse[:, :ROWS, 1] = (-sine * weight).reshape(NLONDEV, ROWS, MODES)
    return (
        forward.reshape(2, MODES, LONS).astype(jnp.bfloat16),
        inverse.reshape(LONS, 2 * MODES).astype(jnp.bfloat16),
    )


def dot(a, b):
    return jnp.dot(a, b, preferred_element_type=F32)


def iota(shape, dim):
    return lax.broadcasted_iota(jnp.int32, shape, dim)


def onehot(condition):
    return jnp.where(condition, 1.0, 0.0).astype(BF16)


def kernel(
    state,
    legendre,
    quad,
    gain,
    skip_weight,
    out_weight,
    assign_s,
    mask_s,
    assign_v,
    base_f,
    base_i,
    out,
    st,
    basis,
    basis_t,
    tbuf,
    ibuf,
    tf,
    ti,
    skipped,
    asrc,
    abuf,
    bsrc,
    inb,
    w,
    fs,
    fs2,
    xin,
    ss,
    csrc,
    ybuf,
    psrc,
    dbuf,
    obuf,
    perm,
    gslab,
    gmix,
    sw,
    ow,
    load_sem,
    state_sem,
    leg_sem,
    out_sem,
    own_sem,
    a_send,
    a_recv,
    b_send,
    b_recv,
    c_send,
    c_recv,
    d_send,
    d_recv,
):
    li = lax.axis_index("lat")
    lo = lax.axis_index("lon")

    def lat_peer(s):
        return lax.rem(li + s, NLATDEV)

    def lon_peer(s):
        return lax.rem(lo + s, NLONDEV)

    slab = pl.multiple_of((lo // 4) * 128, 128)
    loads = [
        pltpu.make_async_copy(base_f, tbuf, load_sem.at[0]),
        pltpu.make_async_copy(base_i, ibuf, load_sem.at[1]),
        pltpu.make_async_copy(gain.at[:, :, pl.ds(slab, 128)], gslab, load_sem.at[2]),
        pltpu.make_async_copy(skip_weight, sw, load_sem.at[3]),
        pltpu.make_async_copy(out_weight, ow, load_sem.at[4]),
    ]

    def state_load(g):
        part = pl.ds(g * LG, LG)
        return pltpu.make_async_copy(state.at[part], st.at[part], state_sem.at[g])

    def basis_load(g):
        part = pl.ds(g * LG, LG)
        return pltpu.make_async_copy(legendre.at[part], basis.at[part], leg_sem.at[g])

    for g in range(GROUPS):
        state_load(g).start()

    barrier = pltpu.get_barrier_semaphore()

    def greet_lon(s, _):
        pl.semaphore_signal(barrier, inc=1, device_id=(li, lon_peer(s)), device_id_type=MESH)
        return 0

    def greet_lat(s, _):
        pl.semaphore_signal(barrier, inc=1, device_id=(lat_peer(s), lo), device_id_type=MESH)
        return 0

    lax.fori_loop(1, NLONDEV, greet_lon, 0)
    lax.fori_loop(1, NLATDEV, greet_lat, 0)

    for copy in loads:
        copy.start()
    for g in range(GROUPS):
        basis_load(g).start()

    row = iota((512, 1024), 0)
    col = iota((512, 1024), 1)
    a_out, half, q_out = col // 256, (col // 128) % 2, (col // CW) % 4
    q_in = jnp.where(half == 0, q_out, q_out + 1 - 2 * (q_out % 2))
    perm[:, 512:1536] = onehot(
        (row // 128 == q_in) & ((row // CW) % 4 == a_out) & (row % CW == col % CW)
    )
    row = iota((512, 512), 0)
    col = iota((512, 512), 1)
    perm[:, 0:512] = onehot(
        (row // 128 == (col // CW) % 4) & ((row // CW) % 4 == col // 128) & (row % CW == col % CW)
    )

    def a_copy(g, s):
        return pltpu.make_async_remote_copy(
            src_ref=asrc.at[g, lon_peer(s)],
            dst_ref=abuf.at[g, lo],
            send_sem=a_send.at[g],
            recv_sem=a_recv.at[g],
            device_id=(li, lon_peer(s)),
            device_id_type=MESH,
        )

    def pack(g, _):
        state_load(g).wait()
        for h in range(2):
            lanes = slice(h * 128, h * 128 + 128)
            x = jnp.concatenate([st[g * LG + a, :, lanes] for a in range(LG)], axis=1)
            y = dot(x, perm[:, 0:512]).astype(BF16)
            for jj in range(4):
                asrc[g, h * 4 + jj, PADDED - 16 : PADDED, :] = jnp.zeros((16, LANES), BF16)
                asrc[g, h * 4 + jj, 0:ROWS, :] = y[:, jj * 128 : jj * 128 + 128]

        @pl.when(g == 0)
        def _():
            pl.semaphore_wait(barrier, NLONDEV + NLATDEV - 2)

        def send(s, _):
            a_copy(g, s).start()
            return 0

        lax.fori_loop(1, NLONDEV, send, 0)
        pltpu.make_async_copy(asrc.at[g, lo], abuf.at[g, lo], own_sem.at[g]).start()
        return 0

    lax.fori_loop(0, GROUPS, pack, 0)

    loads[0].wait()
    pick_t = jnp.where(iota((MODES, MODES), 0) == assign_v[...].reshape(1, MODES), 1.0, 0.0)
    pick = jnp.transpose(pick_t).astype(BF16)
    pick_t = pick_t.astype(BF16)
    for p in range(2):
        for b in range(LONS // 512):
            cols = slice(b * 512, b * 512 + 512)
            tf[p, :, cols] = dot(pick, tbuf[p, :, cols]).astype(BF16)

    lane = iota((1, LANES), 1)

    def b_copy(g, s):
        peer = lat_peer(s)
        return pltpu.make_async_remote_copy(
            src_ref=bsrc.at[g, :, pl.ds(pl.multiple_of(peer * KS, KS), KS), :],
            dst_ref=inb.at[g, li],
            send_sem=b_send.at[g],
            recv_sem=b_recv.at[g],
            device_id=(peer, lo),
            device_id_type=MESH,
        )

    def forward(g):
        pltpu.make_async_copy(
            abuf.at[g, 0 : NLONDEV - 1], abuf.at[g, 0 : NLONDEV - 1], a_recv.at[g]
        ).wait()
        pltpu.make_async_copy(asrc.at[g, lo], abuf.at[g, lo], own_sem.at[g]).wait()
        x = abuf[g].reshape(LONS, LANES)
        scale = jnp.zeros((1, LANES), F32)
        for a in range(LG):
            scale = jnp.where(lane // CW == a, quad[li * LATS + g * LG + a], scale)
        for p in range(2):
            bsrc[g, p] = (dot(tf[p], x) * scale).astype(BF16)

        def send(s, _):
            b_copy(g, s).start()
            return 0

        lax.fori_loop(1, NLATDEV, send, 0)
        inb[g, li] = bsrc[g, :, pl.ds(pl.multiple_of(li * KS, KS), KS), :]

    def prepare(g):
        basis_load(g).wait()
        r = iota((NLAT, NLAT), 0)
        c = iota((NLAT, NLAT), 1)
        order = onehot((r // LATS == c % NLATDEV) & (r % LATS == c // NLATDEV))
        order_t = onehot((c // LATS == r % NLATDEV) & (c % LATS == r // NLATDEV))

        def one(k, _):
            raw = basis[k]
            basis_t[k] = lax.dot_general(
                order_t, raw, (((1,), (1,)), ((), ())), preferred_element_type=F32
            ).astype(BF16)
            basis[k] = dot(raw, order).astype(BF16)
            return 0

        lax.fori_loop(g * 4, g * 4 + 4, one, 0)

    def receive(g):
        pltpu.make_async_copy(
            inb.at[g, 0 : NLATDEV - 1], inb.at[g, 0 : NLATDEV - 1], b_recv.at[g]
        ).wait()
        fs[...] = inb[g].reshape(NLATDEV * 2 * KS, LANES).astype(F32)
        for kk in range(PAIRS):
            for q in range(4):
                start = (q % 2) * KS + 2 * kk + q // 2
                xin[kk * 32 : kk * 32 + 32, q * 128 : q * 128 + 128] = fs[
                    pl.ds(start, 32, stride=32), :
                ].astype(BF16)
        for a in range(LG):
            y = dot(xin[...], perm[:, 512 + a * 256 : 768 + a * 256]).astype(BF16)
            for kk in range(PAIRS):
                w[kk, pl.ds((g * LG + a) * 32, 32), :] = y[kk * 32 : kk * 32 + 32, :]

    forward(0)
    prepare(0)
    forward(1)
    prepare(1)
    forward(2)
    receive(0)
    prepare(2)
    forward(3)
    receive(1)
    prepare(3)

    loads[2].wait()
    for part in range(2):
        x = pltpu.roll(gslab[part], 128 - CW * (lo % 4), 1)
        x = jnp.where(lane < CW, x, 0.0)
        x = x + pltpu.roll(x, CW, 1)
        x = x + pltpu.roll(x, 2 * CW, 1)
        if part == 1:
            x = jnp.where((lane // CW) % 2 == 0, -x, x)
        gmix[part] = x

    loads[1].wait()
    for p in range(2):
        for b in range(LONS // 512):
            rows = slice(b * 512, b * 512 + 512)
            cols = slice(p * MODES, p * MODES + MODES)
            ti[rows, cols] = dot(ibuf[rows, cols], pick_t).astype(BF16)
    loads[3].wait()
    loads[4].wait()

    def skip(a, _):
        skipped[a] = dot(st[a], sw[...])
        return 0

    lax.fori_loop(0, LATS, skip, 0)
    receive(2)
    receive(3)

    def filter_pair(kk, _):
        kept = []
        for k2 in range(2):
            coefficient = dot(basis[2 * kk + k2], w[kk])
            block = assign_s[li * KS + 2 * kk + k2] // LBLK
            parts = []
            for lb in range(LEVELS // LBLK):
                rows = slice(lb * LBLK, lb * LBLK + LBLK)
                live = mask_s[block, lb].astype(F32)
                parts.append(
                    gmix[0, rows, :] * (coefficient[rows, 0:128] * live)
                    + gmix[1, rows, :] * (coefficient[rows, 128:256] * live)
                )
            kept.append(jnp.concatenate(parts, axis=0))
        filtered = jnp.where(lane < 64, kept[0], kept[1]).astype(BF16)
        first = dot(basis_t[2 * kk], filtered)
        second = dot(basis_t[2 * kk + 1], filtered)
        ss[kk] = jnp.where(lane < 64, first, second).astype(BF16)
        return 0

    lax.fori_loop(0, PAIRS, filter_pair, 0)

    def c_copy(g, s):
        peer = lat_peer(s)
        return pltpu.make_async_remote_copy(
            src_ref=csrc.at[g, peer],
            dst_ref=ybuf.at[g, :, pl.ds(pl.multiple_of(li * KS, KS), KS), :],
            send_sem=c_send.at[g],
            recv_sem=c_recv.at[g],
            device_id=(peer, lo),
            device_id_type=MESH,
        )

    def send_back(g, _):
        for kk in range(PAIRS):
            for a in range(LG):
                xin[kk * 32 : kk * 32 + 32, a * 128 : a * 128 + 128] = ss[
                    kk, pl.ds((g * LG + a) * 32, 32), :
                ]
        y = dot(xin[...], perm[:, 0:512])
        for kk in range(PAIRS):
            for q in range(4):
                start = (q % 2) * KS + 2 * kk + q // 2
                fs2[pl.ds(start, 32, stride=32), :] = y[
                    kk * 32 : kk * 32 + 32, q * 128 : q * 128 + 128
                ]
        csrc[g] = fs2[...].astype(BF16).reshape(NLATDEV, 2, KS, LANES)

        def send(s, _):
            c_copy(g, s).start()
            return 0

        lax.fori_loop(1, NLATDEV, send, 0)
        ybuf[g, :, pl.ds(pl.multiple_of(li * KS, KS), KS), :] = csrc[g, li]
        return 0

    lax.fori_loop(0, GROUPS, send_back, 0)

    def d_copy(g, s):
        return pltpu.make_async_remote_copy(
            src_ref=psrc.at[g, lon_peer(s)],
            dst_ref=dbuf.at[g, lo],
            send_sem=d_send.at[g],
            recv_sem=d_recv.at[g],
            device_id=(li, lon_peer(s)),
            device_id_type=MESH,
        )

    def inverse(g):
        pltpu.make_async_copy(
            ybuf.at[g, :, 0 : MODES - KS, :], ybuf.at[g, :, 0 : MODES - KS, :], c_recv.at[g]
        ).wait()
        y = ybuf[g].reshape(2 * MODES, LANES)
        for b in range(NLONDEV // 2):
            rows = slice(b * 2 * PADDED, (b + 1) * 2 * PADDED)
            part = dot(ti[rows, :], y).astype(BF16)
            psrc[g, 2 * b : 2 * b + 2] = part.reshape(2, PADDED, LANES)

        def send(s, _):
            d_copy(g, s).start()
            return 0

        lax.fori_loop(1, NLONDEV, send, 0)
        dbuf[g, lo] = psrc[g, lo]

    def out_store(g):
        part = pl.ds(g * LG, LG)
        return pltpu.make_async_copy(obuf.at[part], out.at[part], out_sem.at[g])

    def mix(g):
        pltpu.make_async_copy(
            dbuf.at[g, 0 : NLONDEV - 1], dbuf.at[g, 0 : NLONDEV - 1], d_recv.at[g]
        ).wait()
        halves = []
        for h in range(2):
            x = jnp.concatenate([dbuf[g, h * 4 + jj] for jj in range(4)], axis=1)
            halves.append(dot(x, perm[:, 0:512]))
        for a in range(LG):
            at = g * LG + a
            lanes = slice(a * 128, a * 128 + 128)
            spatial = jnp.concatenate([half[0:ROWS, lanes] for half in halves], axis=1)
            activated = jax.nn.gelu(spatial + skipped[at], approximate=True).astype(BF16)
            obuf[at] = (st[at].astype(F32) + dot(activated, ow[...])).astype(BF16)
        out_store(g).start()

    inverse(0)
    inverse(1)
    mix(0)
    inverse(2)
    mix(1)
    inverse(3)
    mix(2)
    mix(3)

    for g in range(GROUPS):
        seven = asrc.at[g, 0 : NLONDEV - 1]
        pltpu.make_async_copy(seven, seven, a_send.at[g]).wait()
        others = inb.at[g, 0 : NLATDEV - 1]
        pltpu.make_async_copy(others, others, b_send.at[g]).wait()
        pltpu.make_async_copy(others, others, c_send.at[g]).wait()
        pltpu.make_async_copy(seven, seven, d_send.at[g]).wait()
        out_store(g).wait()


def local(
    state_grid,
    legendre,
    quad_weights,
    spectral_gain,
    skip_weight,
    out_weight,
    assignment,
    tile_mask,
):
    base_f, base_i = base_tables()
    anywhere = pl.BlockSpec(memory_space=pl.ANY)
    smem = pl.BlockSpec(memory_space=pltpu.SMEM)
    vmem = pl.BlockSpec(memory_space=pltpu.VMEM)

    def buf(*shape, dtype=BF16):
        return pltpu.VMEM(shape, dtype)

    sems = pltpu.SemaphoreType.DMA
    return pl.pallas_call(
        kernel,
        out_shape=jax.ShapeDtypeStruct((LATS, ROWS, C), BF16),
        in_specs=[anywhere, anywhere, smem, anywhere, anywhere, anywhere, smem, smem, vmem]
        + [anywhere] * 2,
        out_specs=anywhere,
        scratch_shapes=[
            buf(LATS, ROWS, C),
            buf(KS, LEVELS, NLAT),
            buf(KS, NLAT, LEVELS),
            buf(2, MODES, LONS),
            buf(LONS, 2 * MODES),
            buf(2, MODES, LONS),
            buf(LONS, 2 * MODES),
            buf(LATS, ROWS, C, dtype=F32),
            buf(GROUPS, NLONDEV, PADDED, LANES),
            buf(GROUPS, NLONDEV, PADDED, LANES),
            buf(GROUPS, 2, MODES, LANES),
            buf(GROUPS, NLATDEV, 2, KS, LANES),
            buf(PAIRS, NLAT, 2 * LANES),
            buf(NLATDEV * 2 * KS, LANES, dtype=F32),
            buf(NLATDEV * 2 * KS, LANES, dtype=F32),
            buf(PAIRS * 32, 512),
            buf(PAIRS, NLAT, LANES),
            buf(GROUPS, NLATDEV, 2, KS, LANES),
            buf(GROUPS, 2, MODES, LANES),
            buf(GROUPS, NLONDEV, PADDED, LANES),
            buf(GROUPS, NLONDEV, PADDED, LANES),
            buf(LATS, ROWS, C),
            buf(512, 1536),
            buf(2, LEVELS, 128, dtype=F32),
            buf(2, LEVELS, 128, dtype=F32),
            buf(C, C),
            buf(C, C),
            sems((5,)),
            sems((GROUPS,)),
            sems((GROUPS,)),
            sems((GROUPS,)),
            sems((GROUPS,)),
        ]
        + [sems((GROUPS,))] * 8,
        compiler_params=pltpu.CompilerParams(
            collective_id=0, has_side_effects=True, vmem_limit_bytes=62 * 2**20
        ),
    )(
        state_grid,
        legendre,
        quad_weights,
        spectral_gain,
        skip_weight,
        out_weight,
        assignment,
        tile_mask,
        assignment,
        jnp.asarray(base_f),
        jnp.asarray(base_i),
    )


def solution(mesh):
    in_specs = (P("lat", "lon", None), P("lat", None, None), P(), P(), P(), P(), P(), P())
    out_specs = P("lat", "lon", None)
    return jax.shard_map(local, mesh=mesh, in_specs=in_specs, out_specs=out_specs, check_vma=False)
```

```python
import functools
import math

import jax
import jax.numpy as jnp
import numpy as np
from jax import lax
from jax.experimental import pallas as pl
from jax.experimental.pallas import tpu as pltpu
from jax.sharding import PartitionSpec as P

MESH = pl.DeviceIdType.MESH
F32 = jnp.float32
BF16 = jnp.bfloat16

NLAT, NLON, C = 512, 1440, 256
MODES, LEVELS, LBLK = 512, 512, 128
NLATDEV, NLONDEV = 32, 8
LATS = NLAT // NLATDEV
ROWS = NLON // NLONDEV
PADDED = 192
LONS = PADDED * NLONDEV
KS = MODES // NLATDEV
CW = C // NLONDEV
GROUPS = 4
LG = LATS // GROUPS
LANES = LG * CW
PAIRS = KS // 2
SPLIT_OUT = (3,)
SPLIT_BACK = (0, 1)


def base_tables():
    m = np.arange(MODES, dtype=np.int64)
    n = np.arange(NLON, dtype=np.int64)
    angles = ((n[:, None] * m[None, :]) % NLON) * (2.0 * math.pi / NLON)
    cosine, sine = np.cos(angles), np.sin(angles)
    forward = np.zeros((2, MODES, NLONDEV, PADDED), np.float32)
    forward[0, :, :, :ROWS] = (cosine / NLON).T.reshape(MODES, NLONDEV, ROWS)
    forward[1, :, :, :ROWS] = (-sine / NLON).T.reshape(MODES, NLONDEV, ROWS)
    weight = np.where(m == 0, 1.0, 2.0)[None, :]
    inverse = np.zeros((NLONDEV, PADDED, 2, MODES), np.float32)
    inverse[:, :ROWS, 0] = (cosine * weight).reshape(NLONDEV, ROWS, MODES)
    inverse[:, :ROWS, 1] = (-sine * weight).reshape(NLONDEV, ROWS, MODES)
    return (
        forward.reshape(2, MODES, LONS).astype(jnp.bfloat16),
        inverse.reshape(LONS, 2 * MODES).astype(jnp.bfloat16),
    )


def dot(a, b):
    return jnp.dot(a, b, preferred_element_type=F32)


def iota(shape, dim):
    return lax.broadcasted_iota(jnp.int32, shape, dim)


def onehot(condition):
    return jnp.where(condition, 1.0, 0.0).astype(BF16)


def kernel(
    state,
    legendre,
    quad,
    gain,
    skip_weight,
    out_weight,
    assign_s,
    mask_s,
    assign_v,
    base_f,
    base_i,
    out,
    st,
    st32,
    basis,
    basis_t,
    tbuf,
    ibuf,
    tf,
    ti,
    skipped,
    asrc,
    abuf,
    bsrc,
    inb,
    w,
    fs,
    fs2,
    xin,
    ss,
    csrc,
    ybuf,
    psrc,
    dbuf,
    perm,
    gslab,
    gmix,
    sw,
    ow,
    load_sem,
    state_sem,
    leg_sem,
    out_sem,
    own_sem,
    a_send,
    a_recv,
    b_send,
    b_recv,
    c_send,
    c_recv,
    d_send,
    d_recv,
):
    li = lax.axis_index("lat")
    lo = lax.axis_index("lon")

    def settle(ref, sem):
        with jax.named_scope("wait"):
            pltpu.make_async_copy(ref, ref, sem).wait()

    def lat_peer(s):
        half = (s + 1) // 2
        return lax.rem(li + jnp.where(s % 2 == 1, half, NLATDEV - half), NLATDEV)

    def lon_peer(s):
        return lax.rem(lo + s, NLONDEV)

    slab = pl.multiple_of((lo // 4) * 128, 128)
    loads = [
        pltpu.make_async_copy(base_f, tbuf, load_sem.at[0]),
        pltpu.make_async_copy(base_i, ibuf, load_sem.at[1]),
        pltpu.make_async_copy(gain.at[:, :, pl.ds(slab, 128)], gslab, load_sem.at[2]),
        pltpu.make_async_copy(skip_weight, sw, load_sem.at[3]),
        pltpu.make_async_copy(out_weight, ow, load_sem.at[4]),
    ]

    def state_load(b):
        part = pl.ds(b * (ROWS // 4), ROWS // 4)
        return pltpu.make_async_copy(state.at[part], st.at[part], state_sem.at[b])

    def basis_load(g):
        part = pl.ds(g * LG, LG)
        return pltpu.make_async_copy(legendre.at[part], basis.at[part], leg_sem.at[g])

    for b in range(4):
        state_load(b).start()

    barrier = pltpu.get_barrier_semaphore()

    def greet_lon(s, _):
        pl.semaphore_signal(barrier, inc=1, device_id=(li, lon_peer(s)), device_id_type=MESH)
        return 0

    def greet_lat(s, _):
        pl.semaphore_signal(barrier, inc=1, device_id=(lat_peer(s), lo), device_id_type=MESH)
        return 0

    lax.fori_loop(1, NLONDEV, greet_lon, 0)
    lax.fori_loop(1, NLATDEV, greet_lat, 0)

    for copy in loads:
        copy.start()
    for g in range(GROUPS):
        basis_load(g).start()

    row = iota((512, 1024), 0)
    col = iota((512, 1024), 1)
    a_out, half, q_out = col // 256, (col // 128) % 2, (col // CW) % 4
    q_in = jnp.where(half == 0, q_out, q_out + 1 - 2 * (q_out % 2))
    perm[:, 512:1536] = onehot(
        (row // 128 == q_in) & ((row // CW) % 4 == a_out) & (row % CW == col % CW)
    )
    row = iota((512, 512), 0)
    col = iota((512, 512), 1)
    perm[:, 0:512] = onehot(
        (row // 128 == (col // CW) % 4) & ((row // CW) % 4 == col // 128) & (row % CW == col % CW)
    )

    def a_copy(g, s):
        return pltpu.make_async_remote_copy(
            src_ref=asrc.at[g, lon_peer(s)],
            dst_ref=abuf.at[g, lo],
            send_sem=a_send.at[g],
            recv_sem=a_recv.at[g],
            device_id=(li, lon_peer(s)),
            device_id_type=MESH,
        )

    st32[:, ROWS * LATS :, :] = jnp.zeros((2, (PADDED - ROWS) * LATS, 128), F32)
    for b in range(4):
        state_load(b).wait()
        rows = slice(b * (ROWS // 4), (b + 1) * (ROWS // 4))
        for h in range(2):
            st32[h, rows.start * LATS : rows.stop * LATS, :] = (
                st[rows, :, h * 128 : h * 128 + 128].astype(F32).reshape((ROWS // 4) * LATS, 128)
            )

    def lat_rows(at):
        return pl.ds(at, PADDED, stride=LATS)

    def pack(g):
        for h in range(2):
            x = jnp.concatenate(
                [st32[h, lat_rows(g * LG + a), :].astype(BF16) for a in range(LG)], axis=1
            )
            y = dot(x, perm[:, 0:512]).astype(BF16)
            for jj in range(4):
                asrc[g, h * 4 + jj] = y[:, jj * 128 : jj * 128 + 128]
        if g == 0:
            pl.semaphore_wait(barrier, NLONDEV + NLATDEV - 2)

        def send(s, _):
            a_copy(g, s).start()
            return 0

        lax.fori_loop(1, NLONDEV, send, 0)
        pltpu.make_async_copy(asrc.at[g, lo], abuf.at[g, lo], own_sem.at[g]).start()

    for g in range(GROUPS):
        pack(g)

    loads[0].wait()
    pick_t = jnp.where(iota((MODES, MODES), 0) == assign_v[...].reshape(1, MODES), 1.0, 0.0)
    pick = jnp.transpose(pick_t).astype(BF16)
    pick_t = pick_t.astype(BF16)
    for p in range(2):
        for b in range(LONS // 512):
            cols = slice(b * 512, b * 512 + 512)
            tf[p, :, cols] = dot(pick, tbuf[p, :, cols]).astype(BF16)

    lane = iota((1, LANES), 1)

    def tile(index):
        return pl.ds(pl.multiple_of(index * KS, KS), KS)

    def b_copy(g, s, halves, sem):
        peer = lat_peer(s)
        return pltpu.make_async_remote_copy(
            src_ref=bsrc.at[g, halves, tile(peer), :],
            dst_ref=inb.at[g, halves, tile(li), :],
            send_sem=b_send.at[g, sem],
            recv_sem=b_recv.at[g, sem],
            device_id=(peer, lo),
            device_id_type=MESH,
        )

    def send_all(copy, g, split):
        for sem in range(2 if split else 1):
            halves = sem if split else slice(0, 2)

            def send(s, _, halves=halves, sem=sem):
                copy(g, s, halves, sem).start()
                return 0

            lax.fori_loop(1, NLATDEV, send, 0)

    def settle_all(ref, g, sem, split):
        rows = slice(0, MODES - KS)
        settle(ref.at[g, 0, rows, :] if split else ref.at[g, :, rows, :], sem)

    def forward(g):
        settle(abuf.at[g, 0 : NLONDEV - 1], a_recv.at[g])
        pltpu.make_async_copy(asrc.at[g, lo], abuf.at[g, lo], own_sem.at[g]).wait()
        x = abuf[g].reshape(LONS, LANES)
        scale = jnp.zeros((1, LANES), F32)
        for a in range(LG):
            scale = jnp.where(lane // CW == a, quad[li * LATS + g * LG + a], scale)
        parts = [(dot(tf[p], x) * scale).reshape(NLATDEV, 2, 8, LANES) for p in range(2)]
        for hf in range(2):
            rows = jnp.stack([part[:, hf] for part in parts], axis=1)
            bsrc[g, hf] = rows.reshape(MODES, LANES).astype(BF16)
        send_all(b_copy, g, g in SPLIT_OUT)
        inb[g, :, tile(li), :] = bsrc[g, :, tile(li), :]

    def prepare(g):
        basis_load(g).wait()
        r = iota((NLAT, NLAT), 0)
        c = iota((NLAT, NLAT), 1)
        order = onehot((r // LATS == c % NLATDEV) & (r % LATS == c // NLATDEV))
        order_t = onehot((c // LATS == r % NLATDEV) & (c % LATS == r // NLATDEV))

        def one(k, _):
            raw = basis[k]
            basis_t[k] = lax.dot_general(
                order_t, raw, (((1,), (1,)), ((), ())), preferred_element_type=F32
            ).astype(BF16)
            basis[k] = dot(raw, order).astype(BF16)
            return 0

        lax.fori_loop(g * 4, g * 4 + 4, one, 0)

    def receive(g, hf):
        if g in SPLIT_OUT:
            settle_all(inb, g, b_recv.at[g, hf], True)
        elif hf == 0:
            settle_all(inb, g, b_recv.at[g, 0], False)
        fs[...] = inb[g, hf].astype(F32)
        for kk in range(4):
            for q in range(4):
                start = (q % 2) * 8 + 2 * kk + q // 2
                xin[kk * 32 : kk * 32 + 32, q * 128 : q * 128 + 128] = fs[
                    pl.ds(start, 32, stride=16), :
                ].astype(BF16)
        for a in range(LG):
            y = dot(xin[...], perm[:, 512 + a * 256 : 768 + a * 256]).astype(BF16)
            for kk in range(4):
                w[hf * 4 + kk, pl.ds((g * LG + a) * 32, 32), :] = y[kk * 32 : kk * 32 + 32, :]

    forward(0)
    prepare(0)
    forward(1)
    prepare(1)
    forward(2)
    receive(0, 0)
    receive(0, 1)
    prepare(2)
    forward(3)
    receive(1, 0)
    receive(1, 1)
    prepare(3)

    loads[2].wait()
    for part in range(2):
        x = pltpu.roll(gslab[part], 128 - CW * (lo % 4), 1)
        x = jnp.where(lane < CW, x, 0.0)
        x = x + pltpu.roll(x, CW, 1)
        x = x + pltpu.roll(x, 2 * CW, 1)
        if part == 1:
            x = jnp.where((lane // CW) % 2 == 0, -x, x)
        gmix[part] = x

    loads[1].wait()
    for p in range(2):
        for b in range(LONS // 512):
            rows = slice(b * 512, b * 512 + 512)
            cols = slice(p * MODES, p * MODES + MODES)
            ti[rows, cols] = dot(ibuf[rows, cols], pick_t).astype(BF16)
    loads[3].wait()
    loads[4].wait()

    for a in range(LATS):
        x = jnp.concatenate([st32[h, lat_rows(a), :].astype(BF16) for h in range(2)], axis=1)
        skipped[a] = dot(x, sw[...])

    receive(2, 0)
    receive(2, 1)

    def filter_pair(kk, _):
        kept = []
        for k2 in range(2):
            coefficient = dot(basis[2 * kk + k2], w[kk])
            block = assign_s[li * KS + 2 * kk + k2] // LBLK
            parts = []
            for lb in range(LEVELS // LBLK):
                rows = slice(lb * LBLK, lb * LBLK + LBLK)
                live = mask_s[block, lb].astype(F32)
                parts.append(
                    gmix[0, rows, :] * (coefficient[rows, 0:128] * live)
                    + gmix[1, rows, :] * (coefficient[rows, 128:256] * live)
                )
            kept.append(jnp.concatenate(parts, axis=0))
        filtered = jnp.where(lane < 64, kept[0], kept[1]).astype(BF16)
        first = dot(basis_t[2 * kk], filtered)
        second = dot(basis_t[2 * kk + 1], filtered)
        ss[kk] = jnp.where(lane < 64, first, second).astype(BF16)
        return 0

    def c_copy(g, s, halves, sem):
        peer = lat_peer(s)
        return pltpu.make_async_remote_copy(
            src_ref=csrc.at[g, halves, tile(peer), :],
            dst_ref=ybuf.at[g, halves, tile(li), :],
            send_sem=c_send.at[g, sem],
            recv_sem=c_recv.at[g, sem],
            device_id=(peer, lo),
            device_id_type=MESH,
        )

    def turn(g, hf):
        for kk in range(4):
            for a in range(LG):
                xin[kk * 32 : kk * 32 + 32, a * 128 : a * 128 + 128] = ss[
                    hf * 4 + kk, pl.ds((g * LG + a) * 32, 32), :
                ]
        y = dot(xin[...], perm[:, 0:512])
        for kk in range(4):
            for q in range(4):
                start = (q % 2) * 8 + 2 * kk + q // 2
                fs2[pl.ds(start, 32, stride=16), :] = y[
                    kk * 32 : kk * 32 + 32, q * 128 : q * 128 + 128
                ]
        csrc[g, hf] = fs2[...].astype(BF16)

    def send_half(g, hf):
        turn(g, hf)

        def send(s, _):
            c_copy(g, s, hf, hf).start()
            return 0

        lax.fori_loop(1, NLATDEV, send, 0)

    receive(3, 0)
    lax.fori_loop(0, PAIRS // 2, filter_pair, 0)
    for g in SPLIT_BACK:
        send_half(g, 0)
    receive(3, 1)
    lax.fori_loop(PAIRS // 2, PAIRS, filter_pair, 0)
    for g in SPLIT_BACK:
        send_half(g, 1)
    for g in range(GROUPS):
        if g not in SPLIT_BACK:
            turn(g, 0)
            turn(g, 1)
            send_all(c_copy, g, False)

    def d_copy(g, peer):
        return pltpu.make_async_remote_copy(
            src_ref=psrc.at[g, peer],
            dst_ref=dbuf.at[g, lo],
            send_sem=d_send.at[g],
            recv_sem=d_recv.at[g],
            device_id=(li, peer),
            device_id_type=MESH,
        )

    def inverse(g):
        if g in SPLIT_BACK:
            settle_all(ybuf, g, c_recv.at[g, 0], True)
            settle_all(ybuf, g, c_recv.at[g, 1], True)
        else:
            settle_all(ybuf, g, c_recv.at[g, 0], False)
        ybuf[g, :, tile(li), :] = csrc[g, :, tile(li), :]
        halves = [ybuf[g, hf].astype(F32).reshape(NLATDEV, 2, 8, LANES) for hf in range(2)]
        parts = [
            jnp.stack([half[:, p] for half in halves], axis=1).reshape(MODES, LANES)
            for p in range(2)
        ]
        y = jnp.concatenate(parts, axis=0).astype(BF16)
        for step in (2, 1, 3, 0):
            chip = lax.rem(lo // 2 + step, NLONDEV // 2)
            rows = pl.ds(pl.multiple_of(chip * 2 * PADDED, 2 * PADDED), 2 * PADDED)
            part = dot(ti[rows, :], y).astype(BF16)
            psrc[g, pl.ds(chip * 2, 2)] = part.reshape(2, PADDED, LANES)
            if step:
                d_copy(g, chip * 2).start()
                d_copy(g, chip * 2 + 1).start()
            else:
                d_copy(g, lo + 1 - 2 * (lo % 2)).start()
        dbuf[g, lo] = psrc[g, lo]

    def mix(g):
        settle(dbuf.at[g, 0 : NLONDEV - 1], d_recv.at[g])
        halves = []
        for h in range(2):
            x = jnp.concatenate([dbuf[g, h * 4 + jj] for jj in range(4)], axis=1)
            halves.append(dot(x, perm[:, 0:512]))
        for a in range(LG):
            at = g * LG + a
            lanes = slice(a * 128, a * 128 + 128)
            spatial = jnp.concatenate([half[:, lanes] for half in halves], axis=1)
            activated = jax.nn.gelu(spatial + skipped[at], approximate=True).astype(BF16)
            mixed = dot(activated, ow[...])
            for h in range(2):
                st32[h, lat_rows(at), :] += mixed[:, h * 128 : h * 128 + 128]

    inverse(0)
    inverse(1)
    mix(0)
    inverse(2)
    mix(1)
    inverse(3)
    mix(2)
    mix(3)

    def out_store(b):
        part = pl.ds(b * (ROWS // 4), ROWS // 4)
        return pltpu.make_async_copy(st.at[part], out.at[part], out_sem.at[b])

    for b in range(4):
        rows = slice(b * (ROWS // 4), (b + 1) * (ROWS // 4))
        for h in range(2):
            st[rows, :, h * 128 : h * 128 + 128] = (
                st32[h, rows.start * LATS : rows.stop * LATS, :]
                .reshape(ROWS // 4, LATS, 128)
                .astype(BF16)
            )
        out_store(b).start()

    for g in range(GROUPS):
        settle(asrc.at[g, 0 : NLONDEV - 1], a_send.at[g])
        settle(psrc.at[g, 0 : NLONDEV - 1], d_send.at[g])
        for sem in range(2 if g in SPLIT_OUT else 1):
            settle_all(bsrc, g, b_send.at[g, sem], g in SPLIT_OUT)
        for sem in range(2 if g in SPLIT_BACK else 1):
            settle_all(csrc, g, c_send.at[g, sem], g in SPLIT_BACK)
    for b in range(4):
        out_store(b).wait()


def local(
    state_grid,
    legendre,
    quad_weights,
    spectral_gain,
    skip_weight,
    out_weight,
    assignment,
    tile_mask,
):
    base_f, base_i = base_tables()
    anywhere = pl.BlockSpec(memory_space=pl.ANY)
    smem = pl.BlockSpec(memory_space=pltpu.SMEM)
    vmem = pl.BlockSpec(memory_space=pltpu.VMEM)

    def buf(*shape, dtype=BF16):
        return pltpu.VMEM(shape, dtype)

    sems = pltpu.SemaphoreType.DMA
    result = pl.pallas_call(
        kernel,
        out_shape=jax.ShapeDtypeStruct((ROWS, LATS, C), BF16),
        in_specs=[anywhere, anywhere, smem, anywhere, anywhere, anywhere, smem, smem, vmem]
        + [anywhere] * 2,
        out_specs=anywhere,
        scratch_shapes=[
            buf(ROWS, LATS, C),
            buf(2, PADDED * LATS, 128, dtype=F32),
            buf(KS, LEVELS, NLAT),
            buf(KS, NLAT, LEVELS),
            buf(2, MODES, LONS),
            buf(LONS, 2 * MODES),
            buf(2, MODES, LONS),
            buf(LONS, 2 * MODES),
            buf(LATS, PADDED, C, dtype=F32),
            buf(GROUPS, NLONDEV, PADDED, LANES),
            buf(GROUPS, NLONDEV, PADDED, LANES),
            buf(GROUPS, 2, MODES, LANES),
            buf(GROUPS, 2, MODES, LANES),
            buf(PAIRS, NLAT, 2 * LANES),
            buf(MODES, LANES, dtype=F32),
            buf(MODES, LANES, dtype=F32),
            buf(PAIRS * 16, 512),
            buf(PAIRS, NLAT, LANES),
            buf(GROUPS, 2, MODES, LANES),
            buf(GROUPS, 2, MODES, LANES),
            buf(GROUPS, NLONDEV, PADDED, LANES),
            buf(GROUPS, NLONDEV, PADDED, LANES),
            buf(512, 1536),
            buf(2, LEVELS, 128, dtype=F32),
            buf(2, LEVELS, 128, dtype=F32),
            buf(C, C),
            buf(C, C),
            sems((5,)),
            sems((GROUPS,)),
            sems((GROUPS,)),
            sems((GROUPS,)),
            sems((GROUPS,)),
        ]
        + [sems((GROUPS,))] * 2
        + [sems((GROUPS, 2))] * 4
        + [sems((GROUPS,))] * 2,
        compiler_params=pltpu.CompilerParams(
            collective_id=0, has_side_effects=True, vmem_limit_bytes=62 * 2**20
        ),
    )(
        jnp.transpose(state_grid, (1, 0, 2)),
        legendre,
        quad_weights,
        spectral_gain,
        skip_weight,
        out_weight,
        assignment,
        tile_mask,
        assignment,
        jnp.asarray(base_f),
        jnp.asarray(base_i),
    )
    return jnp.transpose(result, (1, 0, 2))


def solution(mesh):
    in_specs = (P("lat", "lon", None), P("lat", None, None), P(), P(), P(), P(), P(), P())
    out_specs = P("lat", "lon", None)
    return jax.shard_map(local, mesh=mesh, in_specs=in_specs, out_specs=out_specs, check_vma=False)
```

```python
import functools
import math

import jax
import jax.numpy as jnp
import numpy as np
from jax import lax
from jax.experimental import pallas as pl
from jax.experimental.pallas import tpu as pltpu
from jax.sharding import PartitionSpec as P

MESH = pl.DeviceIdType.MESH
F32 = jnp.float32
BF16 = jnp.bfloat16

NLAT, NLON, C = 512, 1440, 256
MODES, LEVELS, LBLK = 512, 512, 128
NLATDEV, NLONDEV = 32, 8
NZ, NX = 8, 4
LATS = NLAT // NLATDEV
ROWS = NLON // NLONDEV
PADDED = 192
BLOCK = PADDED // 2
LONS = PADDED * NLONDEV
KS = MODES // NLATDEV
CW = C // NLONDEV
GROUPS = 4
LG = LATS // GROUPS
LANES = LG * CW
PAIRS = KS // 2
SPLIT_OUT = (2, 3)
SPLIT_BACK = (0, 1)


def base_tables():
    m = np.arange(MODES, dtype=np.int64)
    n = np.arange(NLON, dtype=np.int64)
    angles = ((n[:, None] * m[None, :]) % NLON) * (2.0 * math.pi / NLON)
    cosine, sine = np.cos(angles), np.sin(angles)
    forward = np.zeros((2, MODES, NLONDEV, PADDED), np.float32)
    forward[0, :, :, :ROWS] = (cosine / NLON).T.reshape(MODES, NLONDEV, ROWS)
    forward[1, :, :, :ROWS] = (-sine / NLON).T.reshape(MODES, NLONDEV, ROWS)
    weight = np.where(m == 0, 1.0, 2.0)[None, :]
    inverse = np.zeros((NLONDEV, PADDED, 2, MODES), np.float32)
    inverse[:, :ROWS, 0] = (cosine * weight).reshape(NLONDEV, ROWS, MODES)
    inverse[:, :ROWS, 1] = (-sine * weight).reshape(NLONDEV, ROWS, MODES)
    return (
        forward.reshape(2, MODES, LONS).astype(jnp.bfloat16),
        inverse.reshape(LONS, 2 * MODES).astype(jnp.bfloat16),
    )


def dot(a, b):
    return jnp.dot(a, b, preferred_element_type=F32)


def iota(shape, dim):
    return lax.broadcasted_iota(jnp.int32, shape, dim)


def onehot(condition):
    return jnp.where(condition, 1.0, 0.0).astype(BF16)


def kernel(
    state,
    legendre,
    quad,
    gain,
    skip_weight,
    out_weight,
    assign_s,
    mask_s,
    assign_v,
    base_f,
    base_i,
    out,
    st,
    st32,
    basis,
    tbuf,
    ibuf,
    tf,
    ti,
    skipped,
    asrc,
    abuf,
    bsrc,
    inb,
    w,
    fs,
    fs2,
    xin,
    ss,
    csrc,
    ybuf,
    psrc,
    dbuf,
    perm,
    gslab,
    gmix,
    sw,
    ow,
    load_sem,
    state_sem,
    leg_sem,
    out_sem,
    own_sem,
    a_send,
    a_recv,
    b_send,
    b_recv,
    c_send,
    c_recv,
    d_send,
    d_recv,
):
    li = lax.axis_index("lat")
    lo = lax.axis_index("lon")

    def settle(ref, sem):
        with jax.named_scope("wait"):
            pltpu.make_async_copy(ref, ref, sem).wait()

    my_z, my_x = li // NX, li % NX

    xs = [lax.rem(my_x + dx, NX) for dx in (2, 3, 1, 0)]

    def lat_ring(t, do):
        half = (NZ - t) // 2
        dz = jnp.where(lax.rem(t, 2) == 1, NZ - half, half)
        base = lax.rem(my_z + dz, NZ) * NX
        for peer_x in xs:
            do(base + peer_x)

    def lat_row(do):
        for peer_x in xs[:-1]:
            do(my_z * NX + peer_x)

    def each_lat_peer(do):
        def step(t, _):
            lat_ring(t, do)
            return 0

        lax.fori_loop(0, NZ - 1, step, 0)
        lat_row(do)

    def lon_peer(s):
        return lax.rem(lo + s, NLONDEV)

    slab = pl.multiple_of((lo // 4) * 128, 128)
    loads = [
        pltpu.make_async_copy(base_f, tbuf, load_sem.at[0]),
        pltpu.make_async_copy(base_i, ibuf, load_sem.at[1]),
        pltpu.make_async_copy(gain.at[:, :, pl.ds(slab, 128)], gslab, load_sem.at[2]),
        pltpu.make_async_copy(skip_weight, sw, load_sem.at[3]),
        pltpu.make_async_copy(out_weight, ow, load_sem.at[4]),
    ]

    def state_load(b):
        part = pl.ds(b * (ROWS // 4), ROWS // 4)
        return pltpu.make_async_copy(state.at[part], st.at[part], state_sem.at[b])

    def basis_load(g):
        part = pl.ds(g * LG, LG)
        return pltpu.make_async_copy(legendre.at[part], basis.at[part], leg_sem.at[g])

    for b in range(4):
        state_load(b).start()

    barrier = pltpu.get_barrier_semaphore()

    def greet_lon(s, _):
        pl.semaphore_signal(barrier, inc=1, device_id=(li, lon_peer(s)), device_id_type=MESH)
        return 0

    def greet_lat(peer):
        pl.semaphore_signal(barrier, inc=1, device_id=(peer, lo), device_id_type=MESH)

    lax.fori_loop(1, NLONDEV, greet_lon, 0)
    each_lat_peer(greet_lat)

    for copy in loads:
        copy.start()
    for g in range(GROUPS):
        basis_load(g).start()

    row = iota((512, 512), 0)
    col = iota((512, 512), 1)
    perm[:, 0:512] = onehot(
        (row // 128 == (col // CW) % 4) & ((row // CW) % 4 == col // 128) & (row % CW == col % CW)
    )

    def a_copy(g, s):
        return pltpu.make_async_remote_copy(
            src_ref=asrc.at[g, lon_peer(s)],
            dst_ref=abuf.at[g, lo],
            send_sem=a_send.at[g],
            recv_sem=a_recv.at[g],
            device_id=(li, lon_peer(s)),
            device_id_type=MESH,
        )

    st32[:, ROWS * LATS :, :] = jnp.zeros((2, (PADDED - ROWS) * LATS, 128), F32)
    for b in range(4):
        state_load(b).wait()
        rows = slice(b * (ROWS // 4), (b + 1) * (ROWS // 4))
        for h in range(2):
            st32[h, rows.start * LATS : rows.stop * LATS, :] = (
                st[rows, :, h * 128 : h * 128 + 128].astype(F32).reshape((ROWS // 4) * LATS, 128)
            )

    def lat_rows(at):
        return pl.ds(at, PADDED, stride=LATS)

    def pack(g):
        for h in range(2):
            x = jnp.concatenate(
                [st32[h, lat_rows(g * LG + a), :].astype(BF16) for a in range(LG)], axis=1
            )
            y = dot(x, perm[:, 0:512]).astype(BF16)
            for jj in range(4):
                asrc[g, h * 4 + jj] = y[:, jj * 128 : jj * 128 + 128]
        if g == 0:
            pl.semaphore_wait(barrier, NLONDEV + NLATDEV - 2)

        def send(s, _):
            a_copy(g, s).start()
            return 0

        lax.fori_loop(1, NLONDEV, send, 0)
        pltpu.make_async_copy(asrc.at[g, lo], abuf.at[g, lo], own_sem.at[g]).start()

    for g in range(GROUPS):
        pack(g)

    row = iota((512, 1024), 0)
    col = iota((512, 1024), 1)
    a_out, half, q_out = col // 256, (col // 128) % 2, (col // CW) % 4
    q_in = jnp.where(half == 0, q_out, q_out + 1 - 2 * (q_out % 2))
    perm[:, 512:1536] = onehot(
        (row // 128 == q_in) & ((row // CW) % 4 == a_out) & (row % CW == col % CW)
    )

    loads[0].wait()
    pick_t = jnp.where(iota((MODES, MODES), 0) == assign_v[...].reshape(1, MODES), 1.0, 0.0)
    pick = jnp.transpose(pick_t).astype(BF16)
    pick_t = pick_t.astype(BF16)
    for p in range(2):
        for b in range(LONS // 512):
            cols = slice(b * 512, b * 512 + 512)
            tf[p, :, cols] = dot(pick, tbuf[p, :, cols]).astype(BF16)

    lane = iota((1, LANES), 1)

    def tile(index):
        return pl.ds(pl.multiple_of(index * KS, KS), KS)

    def b_copy(g, peer, halves, sem):
        return pltpu.make_async_remote_copy(
            src_ref=bsrc.at[g, halves, tile(peer), :],
            dst_ref=inb.at[g, halves, tile(li), :],
            send_sem=b_send.at[g, sem],
            recv_sem=b_recv.at[g, sem],
            device_id=(peer, lo),
            device_id_type=MESH,
        )

    def send_both(copy, g):
        each_lat_peer(lambda peer: copy(g, peer, slice(0, 2), 0).start())

    def send_half(copy, g, hf):
        each_lat_peer(lambda peer: copy(g, peer, hf, hf).start())

    def settle_all(ref, g, sem, split):
        rows = slice(0, MODES - KS)
        settle(ref.at[g, 0, rows, :] if split else ref.at[g, :, rows, :], sem)

    def forward(g):
        settle(abuf.at[g, 0 : NLONDEV - 1], a_recv.at[g])
        pltpu.make_async_copy(asrc.at[g, lo], abuf.at[g, lo], own_sem.at[g]).wait()
        x = abuf[g].reshape(LONS, LANES)
        scale = jnp.zeros((1, LANES), F32)
        for a in range(LG):
            scale = jnp.where(lane // CW == a, quad[li * LATS + g * LG + a], scale)
        parts = [(dot(tf[p], x) * scale).reshape(NLATDEV, 2, 8, LANES) for p in range(2)]
        for hf in range(2):
            rows = jnp.stack([part[:, hf] for part in parts], axis=1)
            bsrc[g, hf] = rows.reshape(MODES, LANES).astype(BF16)
        inb[g, :, tile(li), :] = bsrc[g, :, tile(li), :]

    def receive(g, hf):
        if g in SPLIT_OUT:
            settle_all(inb, g, b_recv.at[g, hf], True)
        elif hf == 0:
            settle_all(inb, g, b_recv.at[g, 0], False)
        fs[...] = inb[g, hf].astype(F32)
        for kk in range(4):
            for q in range(4):
                start = (q % 2) * 8 + 2 * kk + q // 2
                xin[kk * 32 : kk * 32 + 32, q * 128 : q * 128 + 128] = fs[
                    pl.ds(start, 32, stride=16), :
                ].astype(BF16)
        for a in range(LG):
            y = dot(xin[...], perm[:, 512 + a * 256 : 768 + a * 256])
            for kk in range(4):
                for half in range(2):
                    w[hf * 4 + kk, half, pl.ds(g * LG + a, 32, stride=LATS), :] = y[
                        kk * 32 : kk * 32 + 32, half * 128 : half * 128 + 128
                    ]

    forward(0)
    send_both(b_copy, 0)
    forward(1)
    send_both(b_copy, 1)
    forward(2)
    send_half(b_copy, 2, 0)
    receive(0, 0)
    receive(0, 1)
    forward(3)
    send_half(b_copy, 3, 0)
    send_half(b_copy, 2, 1)
    send_half(b_copy, 3, 1)
    receive(1, 0)
    receive(1, 1)

    loads[2].wait()
    for part in range(2):
        x = pltpu.roll(gslab[part], 128 - CW * (lo % 4), 1)
        x = jnp.where(lane < CW, x, 0.0)
        x = x + pltpu.roll(x, CW, 1)
        x = x + pltpu.roll(x, 2 * CW, 1)
        if part == 1:
            x = jnp.where((lane // CW) % 2 == 0, -x, x)
        gmix[part] = x

    for g in range(GROUPS):
        basis_load(g).wait()
    receive(2, 0)

    def analyze(kk):
        kept = []
        weighted = jnp.concatenate([w[kk, 0].astype(BF16), w[kk, 1].astype(BF16)], axis=1)
        for k2 in range(2):
            coefficient = dot(basis[2 * kk + k2], weighted)
            block = assign_s[li * KS + 2 * kk + k2] // LBLK
            parts = []
            for lb in range(LEVELS // LBLK):
                rows = slice(lb * LBLK, lb * LBLK + LBLK)
                live = mask_s[block, lb].astype(F32)
                parts.append(
                    gmix[0, rows, :] * (coefficient[rows, 0:128] * live)
                    + gmix[1, rows, :] * (coefficient[rows, 128:256] * live)
                )
            kept.append(jnp.concatenate(parts, axis=0))
        return jnp.transpose(jnp.where(lane < 64, kept[0], kept[1])).astype(BF16)

    def synthesize(kk, filtered):
        parts = [dot(filtered[k2 * 64 : k2 * 64 + 64], basis[2 * kk + k2]) for k2 in range(2)]
        ss[kk] = jnp.transpose(jnp.concatenate(parts, axis=0))

    def legendre_half(hf):
        def step(i, previous):
            synthesize(hf * 4 + i - 1, previous)
            return analyze(hf * 4 + i)

        synthesize(hf * 4 + 3, lax.fori_loop(1, 4, step, analyze(hf * 4)))

    def c_copy(g, peer, halves, sem):
        return pltpu.make_async_remote_copy(
            src_ref=csrc.at[g, halves, tile(peer), :],
            dst_ref=ybuf.at[g, halves, tile(li), :],
            send_sem=c_send.at[g, sem],
            recv_sem=c_recv.at[g, sem],
            device_id=(peer, lo),
            device_id_type=MESH,
        )

    def turn(g, hf):
        for kk in range(4):
            for a in range(LG):
                xin[kk * 32 : kk * 32 + 32, a * 128 : a * 128 + 128] = ss[
                    hf * 4 + kk, pl.ds(g * LG + a, 32, stride=LATS), :
                ].astype(BF16)
        y = dot(xin[...], perm[:, 0:512])
        for kk in range(4):
            for q in range(4):
                start = (q % 2) * 8 + 2 * kk + q // 2
                fs2[pl.ds(start, 32, stride=16), :] = y[
                    kk * 32 : kk * 32 + 32, q * 128 : q * 128 + 128
                ]
        csrc[g, hf] = fs2[...].astype(BF16)

    receive(3, 0)
    legendre_half(0)
    for g in SPLIT_BACK:
        turn(g, 0)
        send_half(c_copy, g, 0)
    receive(2, 1)
    receive(3, 1)
    legendre_half(1)
    for g in SPLIT_BACK:
        turn(g, 1)
        send_half(c_copy, g, 1)
    for g in range(GROUPS):
        if g not in SPLIT_BACK:
            turn(g, 0)
            turn(g, 1)
            send_both(c_copy, g)

    loads[1].wait()
    for p in range(2):
        for b in range(LONS // 512):
            rows = slice(b * 512, b * 512 + 512)
            cols = slice(p * MODES, p * MODES + MODES)
            ti[rows, cols] = dot(ibuf[rows, cols], pick_t).astype(BF16)
    loads[3].wait()
    loads[4].wait()

    for a in range(LATS):
        x = jnp.concatenate([st32[h, lat_rows(a), :].astype(BF16) for h in range(2)], axis=1)
        skipped[a] = dot(x, sw[...])

    def d_copy(g, peer):
        return pltpu.make_async_remote_copy(
            src_ref=psrc.at[g, peer],
            dst_ref=dbuf.at[g, lo],
            send_sem=d_send.at[g],
            recv_sem=d_recv.at[g],
            device_id=(li, peer),
            device_id_type=MESH,
        )

    def inverse(g):
        if g in SPLIT_BACK:
            settle_all(ybuf, g, c_recv.at[g, 0], True)
            settle_all(ybuf, g, c_recv.at[g, 1], True)
        else:
            settle_all(ybuf, g, c_recv.at[g, 0], False)
        ybuf[g, :, tile(li), :] = csrc[g, :, tile(li), :]
        halves = [ybuf[g, hf].astype(F32).reshape(NLATDEV, 2, 8, LANES) for hf in range(2)]
        parts = [
            jnp.stack([half[:, p] for half in halves], axis=1).reshape(MODES, LANES)
            for p in range(2)
        ]
        y = jnp.concatenate(parts, axis=0).astype(BF16)
        for step in (2, 1, 3, 0):
            chip = lax.rem(lo // 2 + step, NLONDEV // 2)
            rows = pl.ds(pl.multiple_of(chip * 2 * PADDED, 2 * PADDED), 2 * PADDED)
            part = dot(ti[rows, :], y).astype(BF16)
            psrc[g, pl.ds(chip * 2, 2)] = part.reshape(2, PADDED, LANES)
            if step:
                d_copy(g, chip * 2).start()
                d_copy(g, chip * 2 + 1).start()
            else:
                d_copy(g, lo + 1 - 2 * (lo % 2)).start()
        dbuf[g, lo] = psrc[g, lo]

    def mix(g):
        settle(dbuf.at[g, 0 : NLONDEV - 1], d_recv.at[g])
        halves = []
        for h in range(2):
            x = jnp.concatenate([dbuf[g, h * 4 + jj] for jj in range(4)], axis=1)
            halves.append(dot(x, perm[:, 0:512]))
        for b in range(2):
            rows = slice(b * BLOCK, b * BLOCK + BLOCK)
            activated = []
            for a in range(LG):
                lanes = slice(a * 128, a * 128 + 128)
                spatial = jnp.concatenate([half[rows, lanes] for half in halves], axis=1)
                skip = skipped[g * LG + a, rows, :]
                activated.append(jax.nn.gelu(spatial + skip, approximate=True).astype(BF16))
            mixed = dot(jnp.concatenate(activated, axis=0), ow[...])
            for a in range(LG):
                at = pl.ds(b * BLOCK * LATS + g * LG + a, BLOCK, stride=LATS)
                for h in range(2):
                    st32[h, at, :] += mixed[
                        a * BLOCK : a * BLOCK + BLOCK, h * 128 : h * 128 + 128
                    ]
            if g == GROUPS - 1:
                first, last = rows.start, min(rows.stop, ROWS)
                for h in range(2):
                    st[first:last, :, h * 128 : h * 128 + 128] = (
                        st32[h, first * LATS : last * LATS, :]
                        .reshape(last - first, LATS, 128)
                        .astype(BF16)
                    )
                out_store(b).start()

    def out_store(b):
        first = b * BLOCK
        part = pl.ds(first, min(first + BLOCK, ROWS) - first)
        return pltpu.make_async_copy(st.at[part], out.at[part], out_sem.at[b])

    inverse(0)
    inverse(1)
    mix(0)
    inverse(2)
    mix(1)
    inverse(3)
    mix(2)
    mix(3)

    for g in range(GROUPS):
        settle(asrc.at[g, 0 : NLONDEV - 1], a_send.at[g])
        settle(psrc.at[g, 0 : NLONDEV - 1], d_send.at[g])
        for sem in range(2 if g in SPLIT_OUT else 1):
            settle_all(bsrc, g, b_send.at[g, sem], g in SPLIT_OUT)
        for sem in range(2 if g in SPLIT_BACK else 1):
            settle_all(csrc, g, c_send.at[g, sem], g in SPLIT_BACK)
    for b in range(2):
        out_store(b).wait()


def local(
    state_grid,
    legendre,
    quad_weights,
    spectral_gain,
    skip_weight,
    out_weight,
    assignment,
    tile_mask,
):
    base_f, base_i = base_tables()
    anywhere = pl.BlockSpec(memory_space=pl.ANY)
    smem = pl.BlockSpec(memory_space=pltpu.SMEM)
    vmem = pl.BlockSpec(memory_space=pltpu.VMEM)

    def buf(*shape, dtype=BF16):
        return pltpu.VMEM(shape, dtype)

    sems = pltpu.SemaphoreType.DMA
    result = pl.pallas_call(
        kernel,
        out_shape=jax.ShapeDtypeStruct((ROWS, LATS, C), BF16),
        in_specs=[anywhere, anywhere, smem, anywhere, anywhere, anywhere, smem, smem, vmem]
        + [anywhere] * 2,
        out_specs=anywhere,
        scratch_shapes=[
            buf(ROWS, LATS, C),
            buf(2, PADDED * LATS, 128, dtype=F32),
            buf(KS, LEVELS, NLAT),
            buf(2, MODES, LONS),
            buf(LONS, 2 * MODES),
            buf(2, MODES, LONS),
            buf(LONS, 2 * MODES),
            buf(LATS, PADDED, C, dtype=F32),
            buf(GROUPS, NLONDEV, PADDED, LANES),
            buf(GROUPS, NLONDEV, PADDED, LANES),
            buf(GROUPS, 2, MODES, LANES),
            buf(GROUPS, 2, MODES, LANES),
            buf(PAIRS, 2, NLAT, LANES, dtype=F32),
            buf(MODES, LANES, dtype=F32),
            buf(MODES, LANES, dtype=F32),
            buf(PAIRS * 16, 512),
            buf(PAIRS, NLAT, LANES, dtype=F32),
            buf(GROUPS, 2, MODES, LANES),
            buf(GROUPS, 2, MODES, LANES),
            buf(GROUPS, NLONDEV, PADDED, LANES),
            buf(GROUPS, NLONDEV, PADDED, LANES),
            buf(512, 1536),
            buf(2, LEVELS, 128, dtype=F32),
            buf(2, LEVELS, 128, dtype=F32),
            buf(C, C),
            buf(C, C),
            sems((5,)),
            sems((GROUPS,)),
            sems((GROUPS,)),
            sems((GROUPS,)),
            sems((GROUPS,)),
        ]
        + [sems((GROUPS,))] * 2
        + [sems((GROUPS, 2))] * 4
        + [sems((GROUPS,))] * 2,
        compiler_params=pltpu.CompilerParams(
            collective_id=0, has_side_effects=True, vmem_limit_bytes=62 * 2**20
        ),
    )(
        jnp.transpose(state_grid, (1, 0, 2)),
        legendre,
        quad_weights,
        spectral_gain,
        skip_weight,
        out_weight,
        assignment,
        tile_mask,
        assignment,
        jnp.asarray(base_f),
        jnp.asarray(base_i),
    )
    return jnp.transpose(result, (1, 0, 2))


def solution(mesh):
    in_specs = (P("lat", "lon", None), P("lat", None, None), P(), P(), P(), P(), P(), P())
    out_specs = P("lat", "lon", None)
    return jax.shard_map(local, mesh=mesh, in_specs=in_specs, out_specs=out_specs, check_vma=False)
```

```python
import functools
import math

import jax
import jax.numpy as jnp
import numpy as np
from jax import lax
from jax.experimental import pallas as pl
from jax.experimental.pallas import tpu as pltpu
from jax.sharding import PartitionSpec as P

MESH = pl.DeviceIdType.MESH
F32 = jnp.float32
BF16 = jnp.bfloat16

NLAT, NLON, C = 512, 1440, 256
MODES, LEVELS, LBLK = 512, 512, 128
NLATDEV, NLONDEV = 32, 8
NZ, NX = 8, 4
LATS = NLAT // NLATDEV
ROWS = NLON // NLONDEV
PADDED = 192
BLOCK = PADDED // 2
LONS = PADDED * NLONDEV
KS = MODES // NLATDEV
CW = C // NLONDEV
GROUPS = 4
LG = LATS // GROUPS
LANES = LG * CW
PAIRS = KS // 2
SPLIT_OUT = (2, 3)
SPLIT_BACK = (0, 1)


def base_tables():
    m = np.arange(MODES, dtype=np.int64)
    n = np.arange(NLON, dtype=np.int64)
    angles = ((n[:, None] * m[None, :]) % NLON) * (2.0 * math.pi / NLON)
    cosine, sine = np.cos(angles), np.sin(angles)
    forward = np.zeros((2, MODES, NLONDEV, PADDED), np.float32)
    forward[0, :, :, :ROWS] = (cosine / NLON).T.reshape(MODES, NLONDEV, ROWS)
    forward[1, :, :, :ROWS] = (-sine / NLON).T.reshape(MODES, NLONDEV, ROWS)
    weight = np.where(m == 0, 1.0, 2.0)[None, :]
    inverse = np.zeros((NLONDEV, PADDED, 2, MODES), np.float32)
    inverse[:, :ROWS, 0] = (cosine * weight).reshape(NLONDEV, ROWS, MODES)
    inverse[:, :ROWS, 1] = (-sine * weight).reshape(NLONDEV, ROWS, MODES)
    return (
        forward.reshape(2, MODES, LONS).astype(jnp.bfloat16),
        inverse.reshape(LONS, 2 * MODES).astype(jnp.bfloat16),
    )


def dot(a, b):
    return jnp.dot(a, b, preferred_element_type=F32)


def iota(shape, dim):
    return lax.broadcasted_iota(jnp.int32, shape, dim)


def onehot(condition):
    return jnp.where(condition, 1.0, 0.0).astype(BF16)


def kernel(
    state,
    legendre,
    quad,
    gain,
    skip_weight,
    out_weight,
    assign_s,
    mask_s,
    assign_v,
    base_f,
    base_i,
    out,
    st,
    st32,
    basis,
    tbuf,
    ibuf,
    tf,
    ti,
    skipped,
    asrc,
    abuf,
    bsrc,
    inb,
    w,
    fs,
    fs2,
    xin,
    ss,
    csrc,
    ybuf,
    psrc,
    dbuf,
    perm,
    gslab,
    gmix,
    sw,
    ow,
    load_sem,
    state_sem,
    leg_sem,
    own_sem,
    a_send,
    a_recv,
    b_send,
    b_recv,
    c_send,
    c_recv,
    d_send,
    d_recv,
):
    li = lax.axis_index("lat")
    lo = lax.axis_index("lon")

    def settle(ref, sem):
        with jax.named_scope("wait"):
            pltpu.make_async_copy(ref, ref, sem).wait()

    my_z, my_x = li // NX, li % NX

    xs = [lax.rem(my_x + dx, NX) for dx in (2, 3, 1, 0)]

    def lat_ring(t, do):
        half = (NZ - t) // 2
        dz = jnp.where(lax.rem(t, 2) == 1, NZ - half, half)
        base = lax.rem(my_z + dz, NZ) * NX
        for peer_x in xs:
            do(base + peer_x)

    def lat_row(do):
        for peer_x in xs[:-1]:
            do(my_z * NX + peer_x)

    def each_lat_peer(do):
        def step(t, _):
            lat_ring(t, do)
            return 0

        lax.fori_loop(0, NZ - 1, step, 0)
        lat_row(do)

    def lon_peer(s):
        return lax.rem(lo + s, NLONDEV)

    slab = pl.multiple_of((lo // 4) * 128, 128)
    loads = [
        pltpu.make_async_copy(base_f, tbuf, load_sem.at[0]),
        pltpu.make_async_copy(base_i, ibuf, load_sem.at[1]),
        pltpu.make_async_copy(gain.at[:, :, pl.ds(slab, 128)], gslab, load_sem.at[2]),
        pltpu.make_async_copy(skip_weight, sw, load_sem.at[3]),
        pltpu.make_async_copy(out_weight, ow, load_sem.at[4]),
    ]

    def state_load(b):
        part = pl.ds(b * (ROWS // 4), ROWS // 4)
        return pltpu.make_async_copy(state.at[part], st.at[part], state_sem.at[b])

    def basis_load(g):
        part = pl.ds(g * LG, LG)
        return pltpu.make_async_copy(legendre.at[part], basis.at[part], leg_sem.at[g])

    for b in range(4):
        state_load(b).start()

    barrier = pltpu.get_barrier_semaphore()

    def greet_lon(s, _):
        pl.semaphore_signal(barrier, inc=1, device_id=(li, lon_peer(s)), device_id_type=MESH)
        return 0

    def greet_lat(peer):
        pl.semaphore_signal(barrier, inc=1, device_id=(peer, lo), device_id_type=MESH)

    lax.fori_loop(1, NLONDEV, greet_lon, 0)
    each_lat_peer(greet_lat)

    for copy in loads:
        copy.start()
    for g in range(GROUPS):
        basis_load(g).start()

    row = iota((512, 512), 0)
    col = iota((512, 512), 1)
    perm[:, 0:512] = onehot(
        (row // 128 == (col // CW) % 4) & ((row // CW) % 4 == col // 128) & (row % CW == col % CW)
    )

    def a_copy(g, s):
        return pltpu.make_async_remote_copy(
            src_ref=asrc.at[g, lon_peer(s)],
            dst_ref=abuf.at[g, lo],
            send_sem=a_send.at[g],
            recv_sem=a_recv.at[g],
            device_id=(li, lon_peer(s)),
            device_id_type=MESH,
        )

    st32[:, ROWS * LATS :, :] = jnp.zeros((2, (PADDED - ROWS) * LATS, 128), F32)
    for b in range(4):
        state_load(b).wait()
        rows = slice(b * (ROWS // 4), (b + 1) * (ROWS // 4))
        for h in range(2):
            st32[h, rows.start * LATS : rows.stop * LATS, :] = (
                st[rows, :, h * 128 : h * 128 + 128].astype(F32).reshape((ROWS // 4) * LATS, 128)
            )

    def lat_rows(at):
        return pl.ds(at, PADDED, stride=LATS)

    def pack(g):
        for h in range(2):
            x = jnp.concatenate(
                [st32[h, lat_rows(g * LG + a), :].astype(BF16) for a in range(LG)], axis=1
            )
            y = dot(x, perm[:, 0:512]).astype(BF16)
            for jj in range(4):
                asrc[g, h * 4 + jj] = y[:, jj * 128 : jj * 128 + 128]
        if g == 0:
            pl.semaphore_wait(barrier, NLONDEV + NLATDEV - 2)

        def send(s, _):
            a_copy(g, s).start()
            return 0

        lax.fori_loop(1, NLONDEV, send, 0)
        pltpu.make_async_copy(asrc.at[g, lo], abuf.at[g, lo], own_sem.at[g]).start()

    for g in range(GROUPS):
        pack(g)

    row = iota((512, 1024), 0)
    col = iota((512, 1024), 1)
    a_out, half, q_out = col // 256, (col // 128) % 2, (col // CW) % 4
    q_in = jnp.where(half == 0, q_out, q_out + 1 - 2 * (q_out % 2))
    perm[:, 512:1536] = onehot(
        (row // 128 == q_in) & ((row // CW) % 4 == a_out) & (row % CW == col % CW)
    )

    loads[0].wait()
    pick_t = jnp.where(iota((MODES, MODES), 0) == assign_v[...].reshape(1, MODES), 1.0, 0.0)
    pick = jnp.transpose(pick_t).astype(BF16)
    pick_t = pick_t.astype(BF16)
    for p in range(2):
        for b in range(LONS // 512):
            cols = slice(b * 512, b * 512 + 512)
            tf[p, :, cols] = dot(pick, tbuf[p, :, cols]).astype(BF16)

    lane = iota((1, LANES), 1)

    def tile(index):
        return pl.ds(pl.multiple_of(index * KS, KS), KS)

    def b_copy(g, peer, halves, sem):
        return pltpu.make_async_remote_copy(
            src_ref=bsrc.at[g, halves, tile(peer), :],
            dst_ref=inb.at[g, halves, tile(li), :],
            send_sem=b_send.at[g, sem],
            recv_sem=b_recv.at[g, sem],
            device_id=(peer, lo),
            device_id_type=MESH,
        )

    def send_both(copy, g):
        each_lat_peer(lambda peer: copy(g, peer, slice(0, 2), 0).start())

    def send_half(copy, g, hf):
        each_lat_peer(lambda peer: copy(g, peer, hf, hf).start())

    def settle_all(ref, g, sem, split):
        rows = slice(0, MODES - KS)
        settle(ref.at[g, 0, rows, :] if split else ref.at[g, :, rows, :], sem)

    def forward(g):
        settle(abuf.at[g, 0 : NLONDEV - 1], a_recv.at[g])
        pltpu.make_async_copy(asrc.at[g, lo], abuf.at[g, lo], own_sem.at[g]).wait()
        x = abuf[g].reshape(LONS, LANES)
        scale = jnp.zeros((1, LANES), F32)
        for a in range(LG):
            scale = jnp.where(lane // CW == a, quad[li * LATS + g * LG + a], scale)
        parts = [(dot(tf[p], x) * scale).reshape(NLATDEV, 2, 8, LANES) for p in range(2)]
        for hf in range(2):
            rows = jnp.stack([part[:, hf] for part in parts], axis=1)
            bsrc[g, hf] = rows.reshape(MODES, LANES).astype(BF16)
        inb[g, :, tile(li), :] = bsrc[g, :, tile(li), :]

    def receive(g, hf):
        if g in SPLIT_OUT:
            settle_all(inb, g, b_recv.at[g, hf], True)
        elif hf == 0:
            settle_all(inb, g, b_recv.at[g, 0], False)
        fs[...] = inb[g, hf].astype(F32)
        for kk in range(4):
            for q in range(4):
                start = (q % 2) * 8 + 2 * kk + q // 2
                xin[kk * 32 : kk * 32 + 32, q * 128 : q * 128 + 128] = fs[
                    pl.ds(start, 32, stride=16), :
                ].astype(BF16)
        for a in range(LG):
            y = dot(xin[...], perm[:, 512 + a * 256 : 768 + a * 256])
            for kk in range(4):
                for half in range(2):
                    w[hf * 4 + kk, half, pl.ds(g * LG + a, 32, stride=LATS), :] = y[
                        kk * 32 : kk * 32 + 32, half * 128 : half * 128 + 128
                    ]

    forward(0)
    send_both(b_copy, 0)
    forward(1)
    send_both(b_copy, 1)
    forward(2)
    send_half(b_copy, 2, 0)
    receive(0, 0)
    receive(0, 1)
    forward(3)
    send_half(b_copy, 3, 0)
    send_half(b_copy, 2, 1)
    send_half(b_copy, 3, 1)
    receive(1, 0)
    receive(1, 1)

    loads[2].wait()
    for part in range(2):
        x = pltpu.roll(gslab[part], 128 - CW * (lo % 4), 1)
        x = jnp.where(lane < CW, x, 0.0)
        x = x + pltpu.roll(x, CW, 1)
        x = x + pltpu.roll(x, 2 * CW, 1)
        if part == 1:
            x = jnp.where((lane // CW) % 2 == 0, -x, x)
        gmix[part] = x

    for g in range(GROUPS):
        basis_load(g).wait()
    receive(2, 0)

    def analyze(kk):
        kept = []
        weighted = jnp.concatenate([w[kk, 0].astype(BF16), w[kk, 1].astype(BF16)], axis=1)
        for k2 in range(2):
            coefficient = dot(basis[2 * kk + k2], weighted)
            block = assign_s[li * KS + 2 * kk + k2] // LBLK
            parts = []
            for lb in range(LEVELS // LBLK):
                rows = slice(lb * LBLK, lb * LBLK + LBLK)
                live = mask_s[block, lb].astype(F32)
                parts.append(
                    gmix[0, rows, :] * (coefficient[rows, 0:128] * live)
                    + gmix[1, rows, :] * (coefficient[rows, 128:256] * live)
                )
            kept.append(jnp.concatenate(parts, axis=0))
        return jnp.transpose(jnp.where(lane < 64, kept[0], kept[1])).astype(BF16)

    def synthesize(kk, filtered):
        parts = [dot(filtered[k2 * 64 : k2 * 64 + 64], basis[2 * kk + k2]) for k2 in range(2)]
        ss[kk] = jnp.transpose(jnp.concatenate(parts, axis=0))

    def legendre_half(hf):
        def step(i, previous):
            synthesize(hf * 4 + i - 1, previous)
            return analyze(hf * 4 + i)

        synthesize(hf * 4 + 3, lax.fori_loop(1, 4, step, analyze(hf * 4)))

    def c_copy(g, peer, halves, sem):
        return pltpu.make_async_remote_copy(
            src_ref=csrc.at[g, halves, tile(peer), :],
            dst_ref=ybuf.at[g, halves, tile(li), :],
            send_sem=c_send.at[g, sem],
            recv_sem=c_recv.at[g, sem],
            device_id=(peer, lo),
            device_id_type=MESH,
        )

    def turn(g, hf):
        for kk in range(4):
            for a in range(LG):
                xin[kk * 32 : kk * 32 + 32, a * 128 : a * 128 + 128] = ss[
                    hf * 4 + kk, pl.ds(g * LG + a, 32, stride=LATS), :
                ].astype(BF16)
        y = dot(xin[...], perm[:, 0:512])
        for kk in range(4):
            for q in range(4):
                start = (q % 2) * 8 + 2 * kk + q // 2
                fs2[pl.ds(start, 32, stride=16), :] = y[
                    kk * 32 : kk * 32 + 32, q * 128 : q * 128 + 128
                ]
        csrc[g, hf] = fs2[...].astype(BF16)

    receive(3, 0)
    legendre_half(0)
    for g in SPLIT_BACK:
        turn(g, 0)
        send_half(c_copy, g, 0)
    receive(2, 1)
    receive(3, 1)
    legendre_half(1)
    for g in SPLIT_BACK:
        turn(g, 1)
        send_half(c_copy, g, 1)
    for g in range(GROUPS):
        if g not in SPLIT_BACK:
            turn(g, 0)
            turn(g, 1)
            send_both(c_copy, g)

    loads[1].wait()
    for p in range(2):
        for b in range(LONS // 512):
            rows = slice(b * 512, b * 512 + 512)
            cols = slice(p * MODES, p * MODES + MODES)
            ti[rows, cols] = dot(ibuf[rows, cols], pick_t).astype(BF16)
    loads[3].wait()
    loads[4].wait()

    for a in range(LATS):
        x = jnp.concatenate([st32[h, lat_rows(a), :].astype(BF16) for h in range(2)], axis=1)
        skipped[a] = dot(x, sw[...])

    def d_copy(g, peer):
        return pltpu.make_async_remote_copy(
            src_ref=psrc.at[g, peer],
            dst_ref=dbuf.at[g, lo],
            send_sem=d_send.at[g],
            recv_sem=d_recv.at[g],
            device_id=(li, peer),
            device_id_type=MESH,
        )

    def inverse(g):
        if g in SPLIT_BACK:
            settle_all(ybuf, g, c_recv.at[g, 0], True)
            settle_all(ybuf, g, c_recv.at[g, 1], True)
        else:
            settle_all(ybuf, g, c_recv.at[g, 0], False)
        ybuf[g, :, tile(li), :] = csrc[g, :, tile(li), :]
        halves = [ybuf[g, hf].astype(F32).reshape(NLATDEV, 2, 8, LANES) for hf in range(2)]
        parts = [
            jnp.stack([half[:, p] for half in halves], axis=1).reshape(MODES, LANES)
            for p in range(2)
        ]
        y = jnp.concatenate(parts, axis=0).astype(BF16)
        for step in (2, 1, 3, 0):
            chip = lax.rem(lo // 2 + step, NLONDEV // 2)
            rows = pl.ds(pl.multiple_of(chip * 2 * PADDED, 2 * PADDED), 2 * PADDED)
            part = dot(ti[rows, :], y).astype(BF16)
            psrc[g, pl.ds(chip * 2, 2)] = part.reshape(2, PADDED, LANES)
            if step:
                d_copy(g, chip * 2).start()
                d_copy(g, chip * 2 + 1).start()
            else:
                d_copy(g, lo + 1 - 2 * (lo % 2)).start()
        dbuf[g, lo] = psrc[g, lo]

    def mix(g):
        settle(dbuf.at[g, 0 : NLONDEV - 1], d_recv.at[g])
        halves = []
        for h in range(2):
            x = jnp.concatenate([dbuf[g, h * 4 + jj] for jj in range(4)], axis=1)
            halves.append(dot(x, perm[:, 0:512]))
        for b in range(2):
            rows = slice(b * BLOCK, b * BLOCK + BLOCK)
            activated = []
            for a in range(LG):
                lanes = slice(a * 128, a * 128 + 128)
                spatial = jnp.concatenate([half[rows, lanes] for half in halves], axis=1)
                skip = skipped[g * LG + a, rows, :]
                activated.append(jax.nn.gelu(spatial + skip, approximate=True).astype(BF16))
            mixed = dot(jnp.concatenate(activated, axis=0), ow[...])
            for a in range(LG):
                at = pl.ds(b * BLOCK * LATS + g * LG + a, BLOCK, stride=LATS)
                for h in range(2):
                    st32[h, at, :] += mixed[
                        a * BLOCK : a * BLOCK + BLOCK, h * 128 : h * 128 + 128
                    ]
            if g == GROUPS - 1:
                first, last = rows.start, min(rows.stop, ROWS)
                for h in range(2):
                    out[first:last, :, h * 128 : h * 128 + 128] = (
                        st32[h, first * LATS : last * LATS, :]
                        .reshape(last - first, LATS, 128)
                        .astype(BF16)
                    )

    inverse(0)
    inverse(1)
    mix(0)
    inverse(2)
    mix(1)
    inverse(3)
    mix(2)
    mix(3)

    for g in range(GROUPS):
        settle(asrc.at[g, 0 : NLONDEV - 1], a_send.at[g])
        settle(psrc.at[g, 0 : NLONDEV - 1], d_send.at[g])
        for sem in range(2 if g in SPLIT_OUT else 1):
            settle_all(bsrc, g, b_send.at[g, sem], g in SPLIT_OUT)
        for sem in range(2 if g in SPLIT_BACK else 1):
            settle_all(csrc, g, c_send.at[g, sem], g in SPLIT_BACK)


def local(
    state_grid,
    legendre,
    quad_weights,
    spectral_gain,
    skip_weight,
    out_weight,
    assignment,
    tile_mask,
):
    base_f, base_i = base_tables()
    anywhere = pl.BlockSpec(memory_space=pl.ANY)
    smem = pl.BlockSpec(memory_space=pltpu.SMEM)
    vmem = pl.BlockSpec(memory_space=pltpu.VMEM)

    def buf(*shape, dtype=BF16):
        return pltpu.VMEM(shape, dtype)

    sems = pltpu.SemaphoreType.DMA
    result = pl.pallas_call(
        kernel,
        out_shape=pltpu.VMEM((ROWS, LATS, C), BF16),
        in_specs=[anywhere, anywhere, smem, anywhere, anywhere, anywhere, smem, smem, vmem]
        + [anywhere] * 2,
        out_specs=vmem,
        scratch_shapes=[
            buf(ROWS, LATS, C),
            buf(2, PADDED * LATS, 128, dtype=F32),
            buf(KS, LEVELS, NLAT),
            buf(2, MODES, LONS),
            buf(LONS, 2 * MODES),
            buf(2, MODES, LONS),
            buf(LONS, 2 * MODES),
            buf(LATS, PADDED, C, dtype=F32),
            buf(GROUPS, NLONDEV, PADDED, LANES),
            buf(GROUPS, NLONDEV, PADDED, LANES),
            buf(GROUPS, 2, MODES, LANES),
            buf(GROUPS, 2, MODES, LANES),
            buf(PAIRS, 2, NLAT, LANES, dtype=F32),
            buf(MODES, LANES, dtype=F32),
            buf(MODES, LANES, dtype=F32),
            buf(PAIRS * 16, 512),
            buf(PAIRS, NLAT, LANES, dtype=F32),
            buf(GROUPS, 2, MODES, LANES),
            buf(GROUPS, 2, MODES, LANES),
            buf(GROUPS, NLONDEV, PADDED, LANES),
            buf(GROUPS, NLONDEV, PADDED, LANES),
            buf(512, 1536),
            buf(2, LEVELS, 128, dtype=F32),
            buf(2, LEVELS, 128, dtype=F32),
            buf(C, C),
            buf(C, C),
            sems((5,)),
            sems((GROUPS,)),
            sems((GROUPS,)),
            sems((GROUPS,)),
        ]
        + [sems((GROUPS,))] * 2
        + [sems((GROUPS, 2))] * 4
        + [sems((GROUPS,))] * 2,
        compiler_params=pltpu.CompilerParams(
            collective_id=0, has_side_effects=True, vmem_limit_bytes=57 * 2**20
        ),
    )(
        jnp.transpose(state_grid, (1, 0, 2)),
        legendre,
        quad_weights,
        spectral_gain,
        skip_weight,
        out_weight,
        assignment,
        tile_mask,
        assignment,
        jnp.asarray(base_f),
        jnp.asarray(base_i),
    )
    return jnp.transpose(result, (1, 0, 2))


def solution(mesh):
    in_specs = (P("lat", "lon", None), P("lat", None, None), P(), P(), P(), P(), P(), P())
    out_specs = P("lat", "lon", None)
    return jax.shard_map(local, mesh=mesh, in_specs=in_specs, out_specs=out_specs, check_vma=False)
```

```python
import functools
import math

import jax
import jax.numpy as jnp
import numpy as np
from jax import lax
from jax.experimental import pallas as pl
from jax.experimental.pallas import tpu as pltpu
from jax.sharding import PartitionSpec as P

MESH = pl.DeviceIdType.MESH
F32 = jnp.float32
BF16 = jnp.bfloat16

NLAT, NLON, C = 512, 1440, 256
MODES, LEVELS, LBLK = 512, 512, 128
NLATDEV, NLONDEV = 32, 8
NZ, NX = 8, 4
LATS = NLAT // NLATDEV
ROWS = NLON // NLONDEV
PADDED = 192
BLOCK = PADDED // 2
LONS = PADDED * NLONDEV
KS = MODES // NLATDEV
CW = C // NLONDEV
GROUPS = 4
LG = LATS // GROUPS
LANES = LG * CW
PAIRS = KS // 2
SPLIT_OUT = (2, 3)
SPLIT_BACK = (0, 1)


def base_tables():
    m = np.arange(MODES, dtype=np.int64)
    n = np.arange(NLON, dtype=np.int64)
    angles = ((n[:, None] * m[None, :]) % NLON) * (2.0 * math.pi / NLON)
    cosine, sine = np.cos(angles), np.sin(angles)
    forward = np.zeros((2, MODES, NLONDEV, PADDED), np.float32)
    forward[0, :, :, :ROWS] = (cosine / NLON).T.reshape(MODES, NLONDEV, ROWS)
    forward[1, :, :, :ROWS] = (-sine / NLON).T.reshape(MODES, NLONDEV, ROWS)
    weight = np.where(m == 0, 1.0, 2.0)[None, :]
    inverse = np.zeros((NLONDEV, PADDED, 2, MODES), np.float32)
    inverse[:, :ROWS, 0] = (cosine * weight).reshape(NLONDEV, ROWS, MODES)
    inverse[:, :ROWS, 1] = (-sine * weight).reshape(NLONDEV, ROWS, MODES)
    return (
        forward.reshape(2, MODES, LONS).astype(jnp.bfloat16),
        inverse.reshape(LONS, 2 * MODES).astype(jnp.bfloat16),
    )


def lane_moves():
    row = np.arange(512)[:, None]
    col = np.arange(512)[None, :]
    swap = (row // 128 == (col // CW) % 4) & ((row // CW) % 4 == col // 128)
    col2 = np.arange(1024)[None, :]
    a_out, half, q_out = col2 // 256, (col2 // 128) % 2, (col2 // CW) % 4
    q_in = np.where(half == 0, q_out, q_out ^ 1)
    both = (row // 128 == q_in) & ((row // CW) % 4 == a_out)
    moves = [swap & (row % CW == col % CW), both & (row % CW == col2 % CW)]
    return np.concatenate(moves, axis=1).astype(jnp.bfloat16)


def dot(a, b):
    return jnp.dot(a, b, preferred_element_type=F32)


def iota(shape, dim):
    return lax.broadcasted_iota(jnp.int32, shape, dim)


def onehot(condition):
    return jnp.where(condition, 1.0, 0.0).astype(BF16)


def kernel(
    state,
    legendre,
    quad,
    gain,
    skip_weight,
    out_weight,
    assign_s,
    mask_s,
    assign_v,
    base_f,
    base_i,
    base_p,
    out,
    st,
    st32,
    basis,
    tbuf,
    ibuf,
    tf,
    ti,
    skipped,
    asrc,
    abuf,
    bsrc,
    inb,
    w,
    fs,
    fs2,
    xin,
    ss,
    csrc,
    ybuf,
    psrc,
    dbuf,
    perm,
    gslab,
    gmix,
    sw,
    ow,
    load_sem,
    state_sem,
    leg_sem,
    own_sem,
    a_send,
    a_recv,
    b_send,
    b_recv,
    c_send,
    c_recv,
    d_send,
    d_recv,
):
    li = lax.axis_index("lat")
    lo = lax.axis_index("lon")

    def settle(ref, sem):
        with jax.named_scope("wait"):
            pltpu.make_async_copy(ref, ref, sem).wait()

    my_z, my_x = li // NX, li % NX

    xs = [lax.rem(my_x + dx, NX) for dx in (2, 3, 1, 0)]

    def lat_ring(t, do):
        half = (NZ - t) // 2
        dz = jnp.where(lax.rem(t, 2) == 1, NZ - half, half)
        base = lax.rem(my_z + dz, NZ) * NX
        for peer_x in xs:
            do(base + peer_x)

    def lat_row(do):
        for peer_x in xs[:-1]:
            do(my_z * NX + peer_x)

    def each_lat_peer(do):
        def step(t, _):
            lat_ring(t, do)
            return 0

        lax.fori_loop(0, NZ - 1, step, 0)
        lat_row(do)

    def lon_peer(s):
        return lax.rem(lo + s, NLONDEV)

    slab = pl.multiple_of((lo // 4) * 128, 128)
    loads = [
        pltpu.make_async_copy(base_f, tbuf, load_sem.at[0]),
        pltpu.make_async_copy(base_i, ibuf, load_sem.at[1]),
        pltpu.make_async_copy(gain.at[:, :, pl.ds(slab, 128)], gslab, load_sem.at[2]),
        pltpu.make_async_copy(skip_weight, sw, load_sem.at[3]),
        pltpu.make_async_copy(out_weight, ow, load_sem.at[4]),
        pltpu.make_async_copy(base_p.at[:, 0:512], perm.at[:, 0:512], load_sem.at[5]),
        pltpu.make_async_copy(base_p.at[:, 512:1536], perm.at[:, 512:1536], load_sem.at[6]),
    ]

    def state_load(b):
        part = pl.ds(b * (ROWS // 4), ROWS // 4)
        return pltpu.make_async_copy(state.at[part], st.at[part], state_sem.at[b])

    def basis_load(g):
        part = pl.ds(g * LG, LG)
        return pltpu.make_async_copy(legendre.at[part], basis.at[part], leg_sem.at[g])

    for b in range(4):
        state_load(b).start()
    loads[5].start()

    barrier = pltpu.get_barrier_semaphore()

    def greet_lon(s, _):
        pl.semaphore_signal(barrier, inc=1, device_id=(li, lon_peer(s)), device_id_type=MESH)
        return 0

    def greet_lat(peer):
        pl.semaphore_signal(barrier, inc=1, device_id=(peer, lo), device_id_type=MESH)

    lax.fori_loop(1, NLONDEV, greet_lon, 0)
    each_lat_peer(greet_lat)

    for copy in loads[:5] + loads[6:]:
        copy.start()
    for g in range(GROUPS):
        basis_load(g).start()

    def a_copy(g, s):
        return pltpu.make_async_remote_copy(
            src_ref=asrc.at[g, lon_peer(s)],
            dst_ref=abuf.at[g, lo],
            send_sem=a_send.at[g],
            recv_sem=a_recv.at[g],
            device_id=(li, lon_peer(s)),
            device_id_type=MESH,
        )

    st32[:, ROWS * LATS :, :] = jnp.zeros((2, (PADDED - ROWS) * LATS, 128), F32)
    for b in range(4):
        state_load(b).wait()
        rows = slice(b * (ROWS // 4), (b + 1) * (ROWS // 4))
        for h in range(2):
            st32[h, rows.start * LATS : rows.stop * LATS, :] = (
                st[rows, :, h * 128 : h * 128 + 128].astype(F32).reshape((ROWS // 4) * LATS, 128)
            )

    def lat_rows(at):
        return pl.ds(at, PADDED, stride=LATS)

    def pack(g):
        if g == 0:
            loads[5].wait()
        for h in range(2):
            x = jnp.concatenate(
                [st32[h, lat_rows(g * LG + a), :].astype(BF16) for a in range(LG)], axis=1
            )
            y = dot(x, perm[:, 0:512]).astype(BF16)
            for jj in range(4):
                asrc[g, h * 4 + jj] = y[:, jj * 128 : jj * 128 + 128]
        if g == 0:
            pl.semaphore_wait(barrier, NLONDEV + NLATDEV - 2)

        def send(s, _):
            a_copy(g, s).start()
            return 0

        lax.fori_loop(1, NLONDEV, send, 0)
        pltpu.make_async_copy(asrc.at[g, lo], abuf.at[g, lo], own_sem.at[g]).start()

    for g in range(GROUPS):
        pack(g)

    loads[6].wait()

    loads[0].wait()
    pick_t = jnp.where(iota((MODES, MODES), 0) == assign_v[...].reshape(1, MODES), 1.0, 0.0)
    pick = jnp.transpose(pick_t).astype(BF16)
    pick_t = pick_t.astype(BF16)
    for p in range(2):
        for b in range(LONS // 512):
            cols = slice(b * 512, b * 512 + 512)
            tf[p, :, cols] = dot(pick, tbuf[p, :, cols]).astype(BF16)

    lane = iota((1, LANES), 1)

    def tile(index):
        return pl.ds(pl.multiple_of(index * KS, KS), KS)

    def b_copy(g, peer, halves, sem):
        return pltpu.make_async_remote_copy(
            src_ref=bsrc.at[g, halves, tile(peer), :],
            dst_ref=inb.at[g, halves, tile(li), :],
            send_sem=b_send.at[g, sem],
            recv_sem=b_recv.at[g, sem],
            device_id=(peer, lo),
            device_id_type=MESH,
        )

    def send_both(copy, g):
        each_lat_peer(lambda peer: copy(g, peer, slice(0, 2), 0).start())

    def send_half(copy, g, hf):
        each_lat_peer(lambda peer: copy(g, peer, hf, hf).start())

    def settle_all(ref, g, sem, split):
        rows = slice(0, MODES - KS)
        settle(ref.at[g, 0, rows, :] if split else ref.at[g, :, rows, :], sem)

    def forward(g):
        settle(abuf.at[g, 0 : NLONDEV - 1], a_recv.at[g])
        pltpu.make_async_copy(asrc.at[g, lo], abuf.at[g, lo], own_sem.at[g]).wait()
        x = abuf[g].reshape(LONS, LANES)
        scale = jnp.zeros((1, LANES), F32)
        for a in range(LG):
            scale = jnp.where(lane // CW == a, quad[li * LATS + g * LG + a], scale)
        parts = [(dot(tf[p], x) * scale).reshape(NLATDEV, 2, 8, LANES) for p in range(2)]
        for hf in range(2):
            rows = jnp.stack([part[:, hf] for part in parts], axis=1)
            bsrc[g, hf] = rows.reshape(MODES, LANES).astype(BF16)
        inb[g, :, tile(li), :] = bsrc[g, :, tile(li), :]

    def receive(g, hf):
        if g in SPLIT_OUT:
            settle_all(inb, g, b_recv.at[g, hf], True)
        elif hf == 0:
            settle_all(inb, g, b_recv.at[g, 0], False)
        fs[...] = inb[g, hf].astype(F32)
        for kk in range(4):
            for q in range(4):
                start = (q % 2) * 8 + 2 * kk + q // 2
                xin[kk * 32 : kk * 32 + 32, q * 128 : q * 128 + 128] = fs[
                    pl.ds(start, 32, stride=16), :
                ].astype(BF16)
        for a in range(LG):
            y = dot(xin[...], perm[:, 512 + a * 256 : 768 + a * 256])
            for kk in range(4):
                for half in range(2):
                    w[hf * 4 + kk, half, pl.ds(g * LG + a, 32, stride=LATS), :] = y[
                        kk * 32 : kk * 32 + 32, half * 128 : half * 128 + 128
                    ]

    forward(0)
    send_both(b_copy, 0)
    forward(1)
    send_both(b_copy, 1)
    forward(2)
    send_half(b_copy, 2, 0)
    receive(0, 0)
    receive(0, 1)
    forward(3)
    send_half(b_copy, 3, 0)
    send_half(b_copy, 2, 1)
    send_half(b_copy, 3, 1)
    receive(1, 0)
    receive(1, 1)

    loads[2].wait()
    for part in range(2):
        x = pltpu.roll(gslab[part], 128 - CW * (lo % 4), 1)
        x = jnp.where(lane < CW, x, 0.0)
        x = x + pltpu.roll(x, CW, 1)
        x = x + pltpu.roll(x, 2 * CW, 1)
        if part == 1:
            x = jnp.where((lane // CW) % 2 == 0, -x, x)
        gmix[part] = x

    for g in range(GROUPS):
        basis_load(g).wait()
    receive(2, 0)

    def analyze(kk):
        kept = []
        weighted = jnp.concatenate([w[kk, 0].astype(BF16), w[kk, 1].astype(BF16)], axis=1)
        for k2 in range(2):
            coefficient = dot(basis[2 * kk + k2], weighted)
            block = assign_s[li * KS + 2 * kk + k2] // LBLK
            parts = []
            for lb in range(LEVELS // LBLK):
                rows = slice(lb * LBLK, lb * LBLK + LBLK)
                live = mask_s[block, lb].astype(F32)
                parts.append(
                    (
                        gmix[0, rows, :] * coefficient[rows, 0:128]
                        + gmix[1, rows, :] * coefficient[rows, 128:256]
                    )
                    * live
                )
            kept.append(jnp.concatenate(parts, axis=0))
        return jnp.transpose(jnp.where(lane < 64, kept[0], kept[1])).astype(BF16)

    def synthesize(kk, filtered):
        parts = [dot(filtered[k2 * 64 : k2 * 64 + 64], basis[2 * kk + k2]) for k2 in range(2)]
        ss[kk] = jnp.transpose(jnp.concatenate(parts, axis=0))

    def legendre_half(hf):
        def step(i, previous):
            synthesize(hf * 4 + i - 1, previous)
            return analyze(hf * 4 + i)

        synthesize(hf * 4 + 3, lax.fori_loop(1, 4, step, analyze(hf * 4)))

    def c_copy(g, peer, halves, sem):
        return pltpu.make_async_remote_copy(
            src_ref=csrc.at[g, halves, tile(peer), :],
            dst_ref=ybuf.at[g, halves, tile(li), :],
            send_sem=c_send.at[g, sem],
            recv_sem=c_recv.at[g, sem],
            device_id=(peer, lo),
            device_id_type=MESH,
        )

    def turn(g, hf):
        for kk in range(4):
            for a in range(LG):
                xin[kk * 32 : kk * 32 + 32, a * 128 : a * 128 + 128] = ss[
                    hf * 4 + kk, pl.ds(g * LG + a, 32, stride=LATS), :
                ].astype(BF16)
        y = dot(xin[...], perm[:, 0:512])
        for kk in range(4):
            for q in range(4):
                start = (q % 2) * 8 + 2 * kk + q // 2
                fs2[pl.ds(start, 32, stride=16), :] = y[
                    kk * 32 : kk * 32 + 32, q * 128 : q * 128 + 128
                ]
        csrc[g, hf] = fs2[...].astype(BF16)

    receive(3, 0)
    legendre_half(0)
    for g in SPLIT_BACK:
        turn(g, 0)
        send_half(c_copy, g, 0)
    receive(2, 1)
    receive(3, 1)
    legendre_half(1)
    for g in SPLIT_BACK:
        turn(g, 1)
        send_half(c_copy, g, 1)
    turn(2, 0)
    turn(2, 1)
    send_both(c_copy, 2)
    turn(3, 0)
    turn(3, 1)

    loads[1].wait()
    for p in range(2):
        for b in range(LONS // 512):
            rows = slice(b * 512, b * 512 + 512)
            cols = slice(p * MODES, p * MODES + MODES)
            ti[rows, cols] = dot(ibuf[rows, cols], pick_t).astype(BF16)
    loads[3].wait()
    loads[4].wait()

    for a in range(LATS):
        x = jnp.concatenate([st32[h, lat_rows(a), :].astype(BF16) for h in range(2)], axis=1)
        skipped[a] = dot(x, sw[...])

    def d_copy(g, peer):
        return pltpu.make_async_remote_copy(
            src_ref=psrc.at[g, peer],
            dst_ref=dbuf.at[g, lo],
            send_sem=d_send.at[g],
            recv_sem=d_recv.at[g],
            device_id=(li, peer),
            device_id_type=MESH,
        )

    def inverse(g):
        if g in SPLIT_BACK:
            settle_all(ybuf, g, c_recv.at[g, 0], True)
            settle_all(ybuf, g, c_recv.at[g, 1], True)
        else:
            settle_all(ybuf, g, c_recv.at[g, 0], False)
        ybuf[g, :, tile(li), :] = csrc[g, :, tile(li), :]
        halves = [ybuf[g, hf].astype(F32).reshape(NLATDEV, 2, 8, LANES) for hf in range(2)]
        parts = [
            jnp.stack([half[:, p] for half in halves], axis=1).reshape(MODES, LANES)
            for p in range(2)
        ]
        y = jnp.concatenate(parts, axis=0).astype(BF16)
        for step in (2, 1, 3, 0):
            chip = lax.rem(lo // 2 + step, NLONDEV // 2)
            rows = pl.ds(pl.multiple_of(chip * 2 * PADDED, 2 * PADDED), 2 * PADDED)
            part = dot(ti[rows, :], y).astype(BF16)
            psrc[g, pl.ds(chip * 2, 2)] = part.reshape(2, PADDED, LANES)
            if step:
                d_copy(g, chip * 2).start()
                d_copy(g, chip * 2 + 1).start()
            else:
                d_copy(g, lo + 1 - 2 * (lo % 2)).start()
        dbuf[g, lo] = psrc[g, lo]

    def mix(g):
        settle(dbuf.at[g, 0 : NLONDEV - 1], d_recv.at[g])
        halves = []
        for h in range(2):
            x = jnp.concatenate([dbuf[g, h * 4 + jj] for jj in range(4)], axis=1)
            halves.append(dot(x, perm[:, 0:512]))
        for b in range(2):
            rows = slice(b * BLOCK, b * BLOCK + BLOCK)
            activated = []
            for a in range(LG):
                lanes = slice(a * 128, a * 128 + 128)
                spatial = jnp.concatenate([half[rows, lanes] for half in halves], axis=1)
                skip = skipped[g * LG + a, rows, :]
                activated.append(jax.nn.gelu(spatial + skip, approximate=True).astype(BF16))
            mixed = dot(jnp.concatenate(activated, axis=0), ow[...])
            for a in range(LG):
                at = pl.ds(b * BLOCK * LATS + g * LG + a, BLOCK, stride=LATS)
                for h in range(2):
                    st32[h, at, :] += mixed[
                        a * BLOCK : a * BLOCK + BLOCK, h * 128 : h * 128 + 128
                    ]
            if g == GROUPS - 1:
                first, last = rows.start, min(rows.stop, ROWS)
                for h in range(2):
                    out[first:last, :, h * 128 : h * 128 + 128] = (
                        st32[h, first * LATS : last * LATS, :]
                        .reshape(last - first, LATS, 128)
                        .astype(BF16)
                    )

    inverse(0)
    send_both(c_copy, 3)
    inverse(1)
    mix(0)
    inverse(2)
    mix(1)
    inverse(3)
    mix(2)
    mix(3)

    for g in range(GROUPS):
        settle(asrc.at[g, 0 : NLONDEV - 1], a_send.at[g])
        settle(psrc.at[g, 0 : NLONDEV - 1], d_send.at[g])
        for sem in range(2 if g in SPLIT_OUT else 1):
            settle_all(bsrc, g, b_send.at[g, sem], g in SPLIT_OUT)
        for sem in range(2 if g in SPLIT_BACK else 1):
            settle_all(csrc, g, c_send.at[g, sem], g in SPLIT_BACK)


def local(
    state_grid,
    legendre,
    quad_weights,
    spectral_gain,
    skip_weight,
    out_weight,
    assignment,
    tile_mask,
):
    base_f, base_i = base_tables()
    anywhere = pl.BlockSpec(memory_space=pl.ANY)
    smem = pl.BlockSpec(memory_space=pltpu.SMEM)
    vmem = pl.BlockSpec(memory_space=pltpu.VMEM)

    def buf(*shape, dtype=BF16):
        return pltpu.VMEM(shape, dtype)

    sems = pltpu.SemaphoreType.DMA
    result = pl.pallas_call(
        kernel,
        out_shape=pltpu.VMEM((ROWS, LATS, C), BF16),
        in_specs=[anywhere, anywhere, smem, anywhere, anywhere, anywhere, smem, smem, vmem]
        + [anywhere] * 3,
        out_specs=vmem,
        scratch_shapes=[
            buf(ROWS, LATS, C),
            buf(2, PADDED * LATS, 128, dtype=F32),
            buf(KS, LEVELS, NLAT),
            buf(2, MODES, LONS),
            buf(LONS, 2 * MODES),
            buf(2, MODES, LONS),
            buf(LONS, 2 * MODES),
            buf(LATS, PADDED, C, dtype=F32),
            buf(GROUPS, NLONDEV, PADDED, LANES),
            buf(GROUPS, NLONDEV, PADDED, LANES),
            buf(GROUPS, 2, MODES, LANES),
            buf(GROUPS, 2, MODES, LANES),
            buf(PAIRS, 2, NLAT, LANES, dtype=F32),
            buf(MODES, LANES, dtype=F32),
            buf(MODES, LANES, dtype=F32),
            buf(PAIRS * 16, 512),
            buf(PAIRS, NLAT, LANES, dtype=F32),
            buf(GROUPS, 2, MODES, LANES),
            buf(GROUPS, 2, MODES, LANES),
            buf(GROUPS, NLONDEV, PADDED, LANES),
            buf(GROUPS, NLONDEV, PADDED, LANES),
            buf(512, 1536),
            buf(2, LEVELS, 128, dtype=F32),
            buf(2, LEVELS, 128, dtype=F32),
            buf(C, C),
            buf(C, C),
            sems((7,)),
            sems((GROUPS,)),
            sems((GROUPS,)),
            sems((GROUPS,)),
        ]
        + [sems((GROUPS,))] * 2
        + [sems((GROUPS, 2))] * 4
        + [sems((GROUPS,))] * 2,
        compiler_params=pltpu.CompilerParams(
            collective_id=0, has_side_effects=True, vmem_limit_bytes=57 * 2**20
        ),
    )(
        jnp.transpose(state_grid, (1, 0, 2)),
        legendre,
        quad_weights,
        spectral_gain,
        skip_weight,
        out_weight,
        assignment,
        tile_mask,
        assignment,
        jnp.asarray(base_f),
        jnp.asarray(base_i),
        jnp.asarray(lane_moves()),
    )
    return jnp.transpose(result, (1, 0, 2))


def solution(mesh):
    in_specs = (P("lat", "lon", None), P("lat", None, None), P(), P(), P(), P(), P(), P())
    out_specs = P("lat", "lon", None)
    return jax.shard_map(local, mesh=mesh, in_specs=in_specs, out_specs=out_specs, check_vma=False)
```
